256 devices in a mesh: walk: 32 (over y, z), det: 8 (over x, core).
Axes of the slice: x: 4, y: 4, z: 8, core: 2. Of those that a mesh axis runs over, the one named last changes fastest.
Arguments:
- positions: float32 [3, 4096, 50], P(None, ('walk', 'det')), may hold values from -6 to 6
- inverse: float32 [4096, 50, 50], P(('walk', 'det')), may hold values from -0.875 to 0.875
- centers: float32 [3, 512], replicated, may hold values from -4 to 4
- exponent: float32 [512], replicated, may hold values from 0.05 to 0.5
- orbital_weights: float32 [512, 128], replicated, may hold values from -0.25 to 0.25
- excitations: int32 [4, 65536], P(None, 'det'), may hold values from 0 to 127, as said below
- state_coeffs: float32 [4, 65536], P(None, 'det'), may hold values from -0.09375 to 0.09375
- local_energy: float32 [4, 4096], P(None, 'walk'), may hold values from -24 to 24
Outputs:
- ci_grad: float32 [4, 8, 8192], P(None, 'det', 'walk')
- state_values: float32 [4, 4096], P(None, ('walk', 'det'))
- state_energy: float32 [4], replicated
The draws below stay inside these ranges and needn't reach their ends.
Inputs may be any that keep to these rules, and one draw needn't show every extreme that they name: `excitations`: rows 0 and 2 are occupied orbitals below 50, rows 1 and 3 virtual orbitals below 128. In each aligned block of 128 determinants rows 0 and 1 are the same; row 2 differs from row 0 and row 3 from row 1.
All inputs are finite; a program needn't handle non-finite values.
Results may differ from the reference program's by a relative error of at most 0.012.
The reference program's roundings to bfloat16 on the way (of `ratio_table`) count: a program that leaves them out, or rounds other values in their place, can miss the bound.
Values may be sent and summed in bfloat16 or wider, within the bound.
No kernel may reach another device: no remote copies, remote signals or barrier semaphores. Data moves between devices by JAX's collectives and lax.ppermute only.
A program may use at most 64 MiB of HBM per device.

```python
import math
import jax
import jax.numpy as jnp
from jax import lax

NEL = 50
V = 128
NBAS = 512
STATES = 4
BLOCK = 128
KD = 8192
W_GROUP = 128
WALKERS = 4096
DETS = 65536
DSHARDS = 8
N_WALK = 32


def draw_excitations(key, part):
    blocks = DETS // BLOCK
    keys = jax.random.split(key, 4)
    parent_row = jax.random.randint(keys[0], (blocks,), 0, NEL)
    parent_col = jax.random.randint(keys[1], (blocks,), 0, V)
    second_row = jax.random.randint(keys[2], (blocks, BLOCK), 0, NEL - 1)
    second_row = second_row + (second_row >= parent_row[:, None]).astype(jnp.int32)
    second_col = jax.random.randint(keys[3], (blocks, BLOCK), 0, V - 1)
    second_col = second_col + (second_col >= parent_col[:, None]).astype(jnp.int32)
    first_row = jnp.broadcast_to(parent_row[:, None], (blocks, BLOCK))
    first_col = jnp.broadcast_to(parent_col[:, None], (blocks, BLOCK))
    return jnp.stack([first_row, first_col, second_row, second_col]).reshape(4, DETS).astype(jnp.int32)


def block_scale(stream_key, extent, cuts, least, largest):
    factor_of, own = 1.0, jax.random.fold_in(stream_key, 6)
    for axis_at, blocks in cuts:
        steps = jnp.exp(jax.random.uniform(jax.random.fold_in(own, axis_at), (blocks,), jnp.float32, least / len(cuts), largest / len(cuts)))
        factor_of = factor_of * jnp.repeat(steps, extent[axis_at] // blocks).reshape([-1 if axis == axis_at else 1 for axis in range(len(extent))])
    return factor_of


def gaussian(rng, shape, spread, reach, cuts=(), dtype=jnp.bfloat16):
    entries = spread * jax.random.normal(rng, shape, jnp.float32)
    if cuts:
        entries = entries * block_scale(rng, shape, cuts, -0.22, 0.18)
    return jnp.clip(entries, -reach, reach).astype(dtype)


def setup_inputs(seed: int = 0) -> dict:
    seeds = jax.random.split(jax.random.key(seed), 9)
    return {
        "positions": gaussian(seeds[0], (3, WALKERS, NEL), 1.0, 6.0, ((1, 256),), jnp.float32),
        "inverse": gaussian(seeds[1], (WALKERS, NEL, NEL), NEL ** -0.5, 0.875, ((0, 256),), jnp.float32),
        "centers": gaussian(seeds[2], (3, NBAS), 1.0, 4.0, (), jnp.float32),
        "exponent": jnp.clip(jnp.exp(jax.random.uniform(seeds[3], (NBAS,), jnp.float32, math.log(0.05), math.log(0.5))), 0.05, 0.5),
        "orbital_weights": gaussian(seeds[4], (NBAS, V), NBAS ** -0.5, 0.25, (), jnp.float32),
        "excitations": draw_excitations(jax.random.fold_in(seeds[8], 71), 0),
        "state_coeffs": gaussian(seeds[6], (STATES, DETS), (DETS // 16) ** -0.5, 0.09375, ((1, 8),), jnp.float32),
        "local_energy": gaussian(seeds[7], (STATES, WALKERS), 4.0, 24.0, ((1, 32),), jnp.float32),
    }


def build_tables(positions, inverse, centers, exponent, orbital_weights):
    distance = jnp.zeros(positions.shape[1:] + (centers.shape[1],), jnp.float32)
    for component in range(3):
        offset = positions[component][:, :, None] - centers[component][None, None, :]
        distance = distance + offset * offset
    basis = jnp.exp(-exponent * distance)
    virtual = jnp.einsum("wem,ma->wea", basis, orbital_weights, precision=lax.Precision.HIGHEST)
    product = jnp.einsum("wie,wea->wia", inverse, virtual, precision=lax.Precision.HIGHEST)
    return product.astype(jnp.bfloat16).reshape(product.shape[0], -1)


def pair_ratios(ratio_table, excitations):
    def pick(rows, cols):
        return jnp.take(ratio_table, rows * V + cols, axis=1).astype(jnp.float32)
    first_row, first_col = excitations[0], excitations[1]
    second_row, second_col = excitations[2], excitations[3]
    return pick(first_row, first_col) * pick(second_row, second_col) - pick(first_row, second_col) * pick(second_row, first_col)


def reference(positions, inverse, centers, exponent, orbital_weights, excitations, state_coeffs, local_energy):
    pos_groups = positions.reshape(3, N_WALK, W_GROUP, NEL).transpose(1, 0, 2, 3)
    inv_groups = inverse.reshape(N_WALK, W_GROUP, NEL, NEL)

    def group_ratios(pos_group, inv_group):
        return pair_ratios(build_tables(pos_group, inv_group, centers, exponent, orbital_weights), excitations)

    def group_values(item):
        ratios = group_ratios(item[0], item[1])
        return lax.dot_general(state_coeffs, ratios, (((1,), (1,)), ((), ())), precision=lax.Precision.HIGHEST)

    values = lax.map(group_values, (pos_groups, inv_groups))
    values = values.transpose(1, 0, 2).reshape(STATES, WALKERS)
    guide = 1.0 + jnp.sum(values * values, axis=0)
    weight = values * values / guide
    scaled = values / guide
    total = jnp.sum(weight, axis=1)
    energy = jnp.sum(weight * local_energy, axis=1) / total
    factor = 2.0 * scaled * (local_energy - energy[:, None]) / total[:, None]
    factor_groups = factor.reshape(STATES, N_WALK, W_GROUP).transpose(1, 0, 2)

    def accumulate(carry, item):
        ratios = group_ratios(item[0], item[1])
        return carry + jnp.dot(item[2], ratios, precision=lax.Precision.HIGHEST), None

    grad, _ = lax.scan(accumulate, jnp.zeros((STATES, DETS), jnp.float32), (pos_groups, inv_groups, factor_groups))
    return grad.reshape(STATES, DSHARDS, KD), values, energy
```

```python
import functools

import jax
import jax.numpy as jnp
from jax import lax
from jax.experimental import pallas as pl
from jax.experimental.pallas import tpu as pltpu
from jax.sharding import PartitionSpec as P

NEL = 50
ROWS = 56
V = 128
NBAS = 512
STATES = 4
BLOCK = 128
OWN = 16
GROUP = 128
KD = 8192
NBLK = KD // BLOCK
PAIRS = NBLK // 2
JP = NEL // 2
NDET = 8
NWALK = 32
JPAD = 64
MIB = 1024 * 1024

F32, BF16 = jnp.float32, jnp.bfloat16
NN = (((1,), (0,)), ((), ()))
NT = (((1,), (1,)), ((), ()))


def dot(a, b, dims=NN):
    return lax.dot_general(a, b, dims, preferred_element_type=F32)


def split(x):
    hi = x.astype(BF16)
    return hi, (x - hi.astype(F32)).astype(BF16)


def vmem(n):
    return [pl.BlockSpec(memory_space=pltpu.VMEM)] * n


def table_kernel(pos_ref, inv_ref, cen_ref, exp_ref, orb_ref, out_ref, pos_s, basis_s, virt_s, inv_s, tab_s):
    pos_s[...] = jnp.zeros_like(pos_s)
    for c in range(3):
        pos_s[c * OWN:(c + 1) * OWN, 0:NEL] = pos_ref[c]
    cols = pos_s[...].T
    neg = -exp_ref[...]
    for w in range(OWN):
        dist = jnp.zeros((ROWS, NBAS), F32)
        for c in range(3):
            off = cols[0:ROWS, c * OWN + w:c * OWN + w + 1] - cen_ref[c:c + 1, :]
            dist = dist + off * off
        basis_s[w * ROWS:(w + 1) * ROWS, :] = jnp.exp(neg * dist)
    b_hi, b_lo = split(basis_s[...])
    o_hi, o_lo = split(orb_ref[...])
    virt_s[...] = jnp.zeros_like(virt_s)
    virt = dot(b_hi, o_hi) + (dot(b_hi, o_lo) + dot(b_lo, o_hi))
    for w in range(OWN):
        virt_s[w, 0:ROWS, :] = virt[w * ROWS:(w + 1) * ROWS]
    inv_s[...] = jnp.zeros_like(inv_s)
    for w in range(OWN):
        inv_s[w, 0:NEL, 0:NEL] = inv_ref[w]
    for w in range(OWN):
        i_hi, i_lo = split(inv_s[w])
        v_hi, v_lo = split(virt_s[w])
        table = dot(i_hi, v_hi) + (dot(i_hi, v_lo) + dot(i_lo, v_hi))
        tab_s[pl.ds(w, ROWS, stride=OWN), :] = table[0:ROWS]
    for i in range(NEL):
        out_ref[i // 2, :, (i % 2) * V:(i % 2 + 1) * V] = tab_s[i * OWN:(i + 1) * OWN, :].astype(BF16)


def prep_kernel(par_ref, exc_ref, coef_ref, chi_ref, clo_ref, obt_ref, ojt_ref, c16_ref, oa_ref, oa_s):
    lane = lax.broadcasted_iota(jnp.int32, (1, V), 1)

    def one_row(blk, _):
        oa_s[pl.ds(blk, 1), :] = jnp.where(lane == par_ref[1, blk], 1.0, 0.0).astype(F32)
        return _

    lax.fori_loop(0, NBLK, one_row, 0)
    oa_ref[...] = oa_s[...].astype(BF16)
    sub_b = lax.broadcasted_iota(jnp.int32, (V, 2 * BLOCK), 0)
    lane_b = lax.broadcasted_iota(jnp.int32, (2 * BLOCK, V), 1)
    half = lax.broadcasted_iota(jnp.int32, (8, 2 * BLOCK), 1) // BLOCK
    upper = lax.broadcasted_iota(jnp.int32, (8, 2 * BLOCK), 0) // STATES

    def quad(q, _):
        parts = []
        for h in range(2):
            at = pl.multiple_of((2 * q + h) * 2 * BLOCK, 2 * BLOCK)
            where = pl.ds(at, 2 * BLOCK)
            j_row, b_row = exc_ref[2:3, where], exc_ref[3:4, where]
            c4 = coef_ref[:, where]
            c8 = jnp.concatenate([c4, c4], axis=0)
            c_hi, c_lo = split(c8)
            c16_ref[:, where] = jnp.concatenate([c_hi.astype(F32), c_lo.astype(F32)], axis=0).astype(BF16)
            own = half == upper
            q_hi = jnp.where(own, c_hi.astype(F32), 0.0)
            q_lo = jnp.where(own, c_lo.astype(F32), 0.0)
            pick_b = jnp.where(sub_b == b_row, 1.0, 0.0).astype(BF16)
            w_hi, w_lo = [], []
            for jp in range(JP):
                m0, m1 = j_row == 2 * jp, j_row == 2 * jp + 1
                w_hi.append(jnp.concatenate([jnp.where(m0, q_hi, 0.0), jnp.where(m1, q_hi, 0.0)], axis=0).astype(BF16))
                w_lo.append(jnp.concatenate([jnp.where(m0, q_lo, 0.0), jnp.where(m1, q_lo, 0.0)], axis=0).astype(BF16))
            parts.append(dot(jnp.concatenate(w_hi, axis=0), pick_b, NT) + dot(jnp.concatenate(w_lo, axis=0), pick_b, NT))
            idx = jnp.concatenate([j_row, b_row, j_row, b_row, j_row, b_row, j_row, b_row], axis=0).astype(F32).T
            obt_ref[where, :] = jnp.where(idx[:, 1:2].astype(jnp.int32) == lane_b, 1.0, 0.0).astype(BF16)
            ojt_ref[where, :] = jnp.where(idx[:, 0:1].astype(jnp.int32) == lane_b, 1.0, 0.0).astype(BF16)
        rows = pl.ds(pl.multiple_of(q * 16, 16), 16)
        for j in range(NEL):
            both = jnp.concatenate([parts[0][j * 8:(j + 1) * 8], parts[1][j * 8:(j + 1) * 8]], axis=0)
            hi, lo = split(both)
            lanes = slice((j % 2) * V, (j % 2 + 1) * V)
            chi_ref[j // 2, rows, lanes] = hi
            clo_ref[j // 2, rows, lanes] = lo
        return _

    lax.fori_loop(0, PAIRS // 2, quad, 0)


def value_kernel(par_ref, me_ref, t0, t1, t2, t3, t4, t5, t6, t7, chi_ref, clo_ref, obt_ref, ojt_ref, c16_ref, oa_ref,
                 part_ref, tab_ref, p_ref, tia_ref, v_s, x_s, acc_s):
    me = me_ref[1]
    for d, t_ref in enumerate((t0, t1, t2, t3, t4, t5, t6, t7)):
        source = jnp.bitwise_xor(me, d)
        tab_ref[:, pl.ds(pl.multiple_of(source * OWN, OWN), OWN), :] = t_ref[...]
    for j in range(NEL, JPAD):
        v_s[pl.ds(j, NBLK, stride=JPAD), :] = jnp.zeros((NBLK, GROUP), F32)
    x_s[...] = jnp.zeros_like(x_s)
    pick_a = oa_ref[...]

    def over_rows(jp, _):
        t = tab_ref[jp]
        x_s[...] += dot(chi_ref[jp], t, NT) + dot(clo_ref[jp], t, NT)
        for j2 in range(2):
            v_s[pl.ds(2 * jp + j2, NBLK, stride=JPAD), :] = dot(pick_a, t[:, j2 * V:(j2 + 1) * V], NT)
        return _

    lax.fori_loop(0, JP, over_rows, 0)

    def own_entry(blk, _):
        row = v_s[pl.ds(blk * JPAD + par_ref[0, blk], 1), :]
        tia_ref[pl.ds(pl.multiple_of(blk * 8, 8), 8), :] = jnp.broadcast_to(row, (8, GROUP))
        return _

    lax.fori_loop(0, NBLK, own_entry, 0)
    acc_s[...] = jnp.zeros_like(acc_s)
    low = lax.broadcasted_iota(jnp.int32, (8, GROUP), 0) < STATES

    def pair(p, first):
        for h in range(2):
            blk = 2 * p + h
            dets = pl.ds(pl.multiple_of(blk * BLOCK, BLOCK), BLOCK)
            i = par_ref[0, blk]
            t_i = tab_ref[lax.shift_right_logical(i, 1), :, pl.ds(pl.multiple_of(jnp.bitwise_and(i, 1) * V, V), V)]
            along = dot(obt_ref[dets, :], t_i, NT)
            column = v_s[pl.ds(pl.multiple_of(blk * JPAD, JPAD), JPAD), :].astype(BF16)
            down = dot(ojt_ref[dets, 0:JPAD], column)
            hi, lo = split(along * down)
            p_ref[dets, 0:GROUP] = hi
            p_ref[dets, GROUP:2 * GROUP] = lo
        both = pl.ds(pl.multiple_of(p * 2 * BLOCK, 2 * BLOCK), 2 * BLOCK)
        acc_s[...] += dot(c16_ref[:, both], p_ref[both, :])
        tia = jnp.where(low, tia_ref[pl.ds(pl.multiple_of(p * 16, 16), 8), :],
                        tia_ref[pl.ds(pl.multiple_of(p * 16 + 8, 8), 8), :])
        return first + x_s[pl.ds(pl.multiple_of(p * 8, 8), 8), :] * tia

    first = lax.fori_loop(0, PAIRS, pair, jnp.zeros((8, GROUP), F32))
    first = first + jnp.concatenate([first[STATES:], first[:STATES]], axis=0)
    second = acc_s[0:8, :] + acc_s[8:16, :]
    part_ref[...] = first - (second[:, 0:GROUP] + second[:, GROUP:2 * GROUP])


def grad_kernel(me_ref, p0, p1, p2, p3, p4, p5, p6, p7, energy_ref, exc_ref, tab_ref, p_ref, tia_ref, *refs):
    val_ref, outs, (g_s, stage_s, order_s) = refs[0], refs[1:1 + NWALK], refs[1 + NWALK:]
    me = me_ref[0]
    for d, part in enumerate((p0, p1, p2, p3, p4, p5, p6, p7)):
        order_s[jnp.bitwise_xor(me_ref[1], d)] = part[...]
    val = order_s[0]
    for d in range(1, NDET):
        val = val + order_s[d]
    val_ref[...] = val
    low = lax.broadcasted_iota(jnp.int32, (8, GROUP), 0) < STATES
    lane = lax.broadcasted_iota(jnp.int32, (8, GROUP), 1)
    square = val * val
    guide = 1.0 + jnp.sum(jnp.where(low, square, 0.0), axis=0, keepdims=True)
    energy = jnp.concatenate([energy_ref[...], energy_ref[...]], axis=0)
    middle = jnp.sum(energy, axis=1, keepdims=True) * (1.0 / GROUP)
    scaled = val / guide
    weight = square / guide
    sums = jnp.sum(jnp.where(low, weight, weight * energy), axis=1, keepdims=True)
    meta = jnp.where(lane == 0, sums, jnp.where(lane == 1, middle, 0.0))
    factor = jnp.where(low, scaled * (energy - middle), scaled)
    f_hi, f_lo = split(factor)
    f16 = jnp.concatenate([f_hi.astype(F32), f_lo.astype(F32)], axis=0).astype(BF16)
    f16 = jnp.concatenate([f16, f16], axis=1)
    lhs = tia_ref[...].reshape(NBLK, 8, GROUP) * factor[None]
    l_hi, l_lo = split(lhs.reshape(NBLK * 8, GROUP))
    lhs = jnp.concatenate([l_hi, l_lo], axis=1)

    def over_rows(jp, _):
        t = tab_ref[jp]
        g = dot(lhs, jnp.concatenate([t, t], axis=0)).reshape(NBLK, 8, 2 * V)
        hi, lo = split(jnp.concatenate([g[:, :, 0:V], g[:, :, V:2 * V]], axis=1))
        rows = pl.ds(pl.multiple_of(jp * 16, 16), 16)
        g_s[:, rows, 0:V] = hi
        g_s[:, rows, V:2 * V] = lo
        return _

    lax.fori_loop(0, JP, over_rows, 0)
    sub_b = lax.broadcasted_iota(jnp.int32, (V, BLOCK), 0)

    def slot(d, _):
        p = jnp.bitwise_and(me + d, NWALK - 1)
        both = pl.ds(pl.multiple_of(p * 2 * BLOCK, 2 * BLOCK), 2 * BLOCK)
        second = dot(f16, p_ref[both, :], NT)
        second = second[0:8] + second[8:16]
        for h in range(2):
            dets = pl.ds(pl.multiple_of(p * 2 * BLOCK + h * BLOCK, BLOCK), BLOCK)
            j_row, b_row = exc_ref[2:3, dets], exc_ref[3:4, dets]
            pick_b = jnp.where(sub_b == b_row, 1.0, 0.0).astype(BF16)
            y = dot(g_s[2 * p + h], jnp.concatenate([pick_b, pick_b], axis=0))
            first = jnp.zeros((8, BLOCK), F32)
            for j in range(NEL):
                first = jnp.where(j_row == j, y[j * 8:(j + 1) * 8], first)
            stage_s[d, :, h * BLOCK:(h + 1) * BLOCK] = first - second[:, h * BLOCK:(h + 1) * BLOCK]
        stage_s[d, :, 2 * BLOCK:3 * BLOCK] = meta
        return _

    lax.fori_loop(0, NWALK, slot, 0)
    for d in range(NWALK):
        outs[d][...] = stage_s[d]


def final_kernel(me_ref, *refs):
    ins, (grad_ref, energy_ref, order_s) = refs[:NWALK], refs[NWALK:]
    for d in range(NWALK):
        order_s[jnp.bitwise_and(me_ref[0] - d + NWALK, NWALK - 1)] = ins[d][:, 256:384]
    meta = order_s[0]
    for d in range(1, NWALK):
        meta = meta + order_s[d]
    total, weighted = meta[0:STATES, 0:1], meta[STATES:8, 0:1]
    energy = weighted / total
    grad = jnp.zeros((STATES, 256), F32)
    for d in range(NWALK):
        grad = grad + (ins[d][0:STATES, 0:256] + (ins[d][0:STATES, 257:258] - energy) * ins[d][STATES:8, 0:256])
    grad_ref[...] = 2.0 * grad / total
    energy_ref[...] = jnp.broadcast_to(energy, (STATES, 128))


def params(mib):
    return pltpu.CompilerParams(vmem_limit_bytes=mib * MIB)


def make_table(positions, inverse, centers, exponent, orbital_weights):
    return pl.pallas_call(
        table_kernel,
        out_shape=jax.ShapeDtypeStruct((JP, OWN, 2 * V), BF16),
        in_specs=vmem(5), out_specs=vmem(1)[0],
        scratch_shapes=[pltpu.VMEM((128, 128), F32), pltpu.VMEM((OWN * ROWS, NBAS), F32),
                        pltpu.VMEM((OWN, 128, V), F32), pltpu.VMEM((OWN, JPAD, 128), F32),
                        pltpu.VMEM((ROWS * OWN, V), F32)],
        compiler_params=params(24), name="tables",
    )(positions, inverse, centers, exponent.reshape(1, NBAS), orbital_weights)


def prepare(parents, excitations, coeffs):
    return pl.pallas_call(
        prep_kernel,
        out_shape=[jax.ShapeDtypeStruct((JP, NBLK * STATES, 2 * V), BF16)] * 2
        + [jax.ShapeDtypeStruct((KD, V), BF16)] * 2
        + [jax.ShapeDtypeStruct((16, KD), BF16), jax.ShapeDtypeStruct((NBLK, V), BF16)],
        in_specs=[pl.BlockSpec(memory_space=pltpu.SMEM)] + vmem(2), out_specs=vmem(6),
        scratch_shapes=[pltpu.VMEM((NBLK, V), F32)],
        compiler_params=params(24), name="prepare",
    )(parents, excitations, coeffs)


def partial_values(parents, me, tables, prepared):
    return pl.pallas_call(
        value_kernel,
        out_shape=[jax.ShapeDtypeStruct((8, GROUP), F32), jax.ShapeDtypeStruct((JP, GROUP, 2 * V), BF16),
                   jax.ShapeDtypeStruct((KD, 2 * GROUP), BF16), jax.ShapeDtypeStruct((NBLK * 8, GROUP), F32)],
        in_specs=[pl.BlockSpec(memory_space=pltpu.SMEM)] * 2 + vmem(NDET + 6), out_specs=vmem(4),
        scratch_shapes=[pltpu.VMEM((NBLK * JPAD, GROUP), F32), pltpu.VMEM((NBLK * STATES, GROUP), F32),
                        pltpu.VMEM((16, 2 * GROUP), F32)],
        compiler_params=params(32), name="partial_values",
    )(parents, me, *tables, *prepared)


def gradient(me, parts, local_energy, excitations, tab, pair_products, tia):
    return pl.pallas_call(
        grad_kernel,
        out_shape=[jax.ShapeDtypeStruct((8, GROUP), F32)] + [jax.ShapeDtypeStruct((8, 384), F32)] * NWALK,
        in_specs=[pl.BlockSpec(memory_space=pltpu.SMEM)] + vmem(NDET + 5), out_specs=vmem(1 + NWALK),
        scratch_shapes=[pltpu.VMEM((NBLK, JP * 16, 2 * V), BF16), pltpu.VMEM((NWALK, 8, 384), F32),
                        pltpu.VMEM((NDET, 8, GROUP), F32)],
        compiler_params=params(40), name="gradient",
    )(me, *parts, local_energy, excitations, tab, pair_products, tia)


def finish(me, messages):
    return pl.pallas_call(
        final_kernel,
        out_shape=[jax.ShapeDtypeStruct((STATES, 256), F32), jax.ShapeDtypeStruct((STATES, 128), F32)],
        in_specs=[pl.BlockSpec(memory_space=pltpu.SMEM)] + vmem(NWALK), out_specs=vmem(2),
        scratch_shapes=[pltpu.VMEM((NWALK, 8, 128), F32)],
        compiler_params=params(8), name="finish",
    )(me, *messages)


def to_group(x):
    return [x] + [lax.ppermute(x, "det", [(i, i ^ d) for i in range(NDET)]) for d in range(1, NDET)]


def shards(positions, inverse, centers, exponent, orbital_weights, excitations, state_coeffs, local_energy):
    det, walk = lax.axis_index("det"), lax.axis_index("walk")
    tables = to_group(make_table(positions, inverse, centers, exponent, orbital_weights))
    me = jnp.stack([walk, det])
    parents = excitations[0:2, ::BLOCK]
    prepared = prepare(parents, excitations, state_coeffs)
    part, tab, products, tia = partial_values(parents, me, tables, prepared)
    values, *messages = gradient(me, to_group(part), local_energy, excitations, tab, products, tia)
    arrived = [messages[0]]
    for d in range(1, NWALK):
        arrived.append(lax.ppermute(messages[d], "walk", [(i, (i + d) % NWALK) for i in range(NWALK)]))
    grad, energy = finish(me, arrived)
    own = lax.dynamic_slice_in_dim(values[0:STATES], det * OWN, OWN, 1)
    return grad[:, None, :], own, energy[:, 0]


def solution(mesh):
    in_specs = (
        P(None, ("walk", "det"), None),
        P(("walk", "det"), None, None),
        P(),
        P(),
        P(),
        P(None, "det"),
        P(None, "det"),
        P(None, "walk"),
    )
    out_specs = (P(None, "det", "walk"), P(None, ("walk", "det")), P())
    return jax.shard_map(shards, mesh=mesh, in_specs=in_specs, out_specs=out_specs, check_vma=False)
```

```python
import jax
import jax.numpy as jnp
from jax import lax
from jax.experimental import pallas as pl
from jax.experimental.pallas import tpu as pltpu
from jax.sharding import PartitionSpec as P

NEL = 50
ROWS = 56
V = 128
NBAS = 512
STATES = 4
BLOCK = 128
OWN = 16
GROUP = 128
KD = 8192
NBLK = KD // BLOCK
PAIRS = NBLK // 2
JP = NEL // 2
NDET = 8
NWALK = 32
JPAD = 64
MIB = 1024 * 1024

F32, BF16 = jnp.float32, jnp.bfloat16
NN = (((1,), (0,)), ((), ()))
NT = (((1,), (1,)), ((), ()))


def dot(a, b, dims=NN):
    return lax.dot_general(a, b, dims, preferred_element_type=F32)


def split(x):
    hi = x.astype(BF16)
    return hi, (x - hi.astype(F32)).astype(BF16)


def vmem(n):
    return [pl.BlockSpec(memory_space=pltpu.VMEM)] * n


def table_kernel(pos_hbm, inv_hbm, cen_hbm, exp_hbm, orb_hbm, out_ref, pos_ref, inv_ref, cen_ref, exp_ref, orb_ref,
                 pos_s, basis_s, virt_s, inv_s, tab_s, sems):
    copies = [pltpu.make_async_copy(src, dst, sems.at[n]) for n, (src, dst) in enumerate(
        ((pos_hbm, pos_ref), (cen_hbm, cen_ref), (exp_hbm, exp_ref), (orb_hbm, orb_ref), (inv_hbm, inv_ref)))]
    for copy in copies:
        copy.start()
    pos_s[...] = jnp.zeros_like(pos_s)
    virt_s[...] = jnp.zeros_like(virt_s)
    inv_s[...] = jnp.zeros_like(inv_s)
    for copy in copies[:3]:
        copy.wait()
    for c in range(3):
        pos_s[c * OWN:(c + 1) * OWN, 0:NEL] = pos_ref[c]
    cols = pos_s[...].T
    neg = -exp_ref[...]
    for w in range(OWN):
        dist = jnp.zeros((ROWS, NBAS), F32)
        for c in range(3):
            off = cols[0:ROWS, c * OWN + w:c * OWN + w + 1] - cen_ref[c:c + 1, :]
            dist = dist + off * off
        basis_s[w * ROWS:(w + 1) * ROWS, :] = jnp.exp(neg * dist)
    b_hi, b_lo = split(basis_s[...])
    copies[3].wait()
    o_hi, o_lo = split(orb_ref[...])
    virt = dot(b_hi, o_hi) + (dot(b_hi, o_lo) + dot(b_lo, o_hi))
    for w in range(OWN):
        virt_s[w, 0:ROWS, :] = virt[w * ROWS:(w + 1) * ROWS]
    copies[4].wait()
    for w in range(OWN):
        inv_s[w, 0:NEL, 0:NEL] = inv_ref[:, w, :]
    for w in range(OWN):
        i_hi, i_lo = split(inv_s[w])
        v_hi, v_lo = split(virt_s[w])
        table = dot(i_hi, v_hi) + (dot(i_hi, v_lo) + dot(i_lo, v_hi))
        tab_s[pl.ds(w, ROWS, stride=OWN), :] = table[0:ROWS]
    for i in range(NEL):
        out_ref[i // 2, :, (i % 2) * V:(i % 2 + 1) * V] = tab_s[i * OWN:(i + 1) * OWN, :].astype(BF16)


def picks_kernel(exc_smem, exc_ref, coef_ref, obt_ref, ojt_ref, c16_ref, oa_ref, oa_s):
    lane = lax.broadcasted_iota(jnp.int32, (1, V), 1)

    def one_row(blk, _):
        oa_s[pl.ds(blk, 1), :] = jnp.where(lane == exc_smem[1, blk * BLOCK], 1.0, 0.0).astype(F32)
        return _

    lax.fori_loop(0, NBLK, one_row, 0)
    oa_ref[...] = oa_s[...].astype(BF16)
    lane_b = lax.broadcasted_iota(jnp.int32, (2 * BLOCK, V), 1)

    def pair(p, _):
        where = pl.ds(pl.multiple_of(p * 2 * BLOCK, 2 * BLOCK), 2 * BLOCK)
        c4 = coef_ref[:, where]
        c_hi, c_lo = split(jnp.concatenate([c4, c4], axis=0))
        c16_ref[:, where] = jnp.concatenate([c_hi.astype(F32), c_lo.astype(F32)], axis=0).astype(BF16)
        both = exc_ref[2:4, where]
        idx = jnp.concatenate([both, both, both, both], axis=0).astype(F32).T
        obt_ref[where, :] = jnp.where(idx[:, 1:2].astype(jnp.int32) == lane_b, 1.0, 0.0).astype(BF16)
        ojt_ref[where, :] = jnp.where(idx[:, 0:1].astype(jnp.int32) == lane_b, 1.0, 0.0).astype(BF16)
        return _

    lax.fori_loop(0, PAIRS, pair, 0)


def spread_kernel(exc_ref, coef_ref, chi_ref, clo_ref):
    sub_b = lax.broadcasted_iota(jnp.int32, (V, 2 * BLOCK), 0)
    half = lax.broadcasted_iota(jnp.int32, (8, 2 * BLOCK), 1) // BLOCK
    upper = lax.broadcasted_iota(jnp.int32, (8, 2 * BLOCK), 0) // STATES

    def quad(q, _):
        parts = []
        for h in range(2):
            where = pl.ds(pl.multiple_of((2 * q + h) * 2 * BLOCK, 2 * BLOCK), 2 * BLOCK)
            j_row, b_row = exc_ref[2:3, where], exc_ref[3:4, where]
            c4 = coef_ref[:, where]
            c_hi, c_lo = split(jnp.concatenate([c4, c4], axis=0))
            own = half == upper
            q_hi = jnp.where(own, c_hi.astype(F32), 0.0)
            q_lo = jnp.where(own, c_lo.astype(F32), 0.0)
            pick_b = jnp.where(sub_b == b_row, 1.0, 0.0).astype(BF16)
            w_hi, w_lo = [], []
            for jp in range(JP):
                m0, m1 = j_row == 2 * jp, j_row == 2 * jp + 1
                w_hi.append(jnp.concatenate([jnp.where(m0, q_hi, 0.0), jnp.where(m1, q_hi, 0.0)], axis=0).astype(BF16))
                w_lo.append(jnp.concatenate([jnp.where(m0, q_lo, 0.0), jnp.where(m1, q_lo, 0.0)], axis=0).astype(BF16))
            parts.append(dot(jnp.concatenate(w_hi, axis=0), pick_b, NT) + dot(jnp.concatenate(w_lo, axis=0), pick_b, NT))
        rows = pl.ds(pl.multiple_of(q * 16, 16), 16)
        for j in range(NEL):
            both = jnp.concatenate([parts[0][j * 8:(j + 1) * 8], parts[1][j * 8:(j + 1) * 8]], axis=0)
            hi, lo = split(both)
            lanes = slice((j % 2) * V, (j % 2 + 1) * V)
            chi_ref[j // 2, rows, lanes] = hi
            clo_ref[j // 2, rows, lanes] = lo
        return _

    lax.fori_loop(0, PAIRS // 2, quad, 0)


def value_kernel(exc_smem, me_ref, t0, t1, t2, t3, t4, t5, t6, t7, chi_ref, clo_ref, obt_ref, ojt_ref, c16_ref, oa_ref,
                 part_ref, tab_ref, p_ref, tia_ref, v_s, x_s, acc_s):
    x, c = lax.shift_right_logical(me_ref[1], 1), jnp.bitwise_and(me_ref[1], 1)
    ahead = 1 - 2 * c
    sources = ((x, c), (x - ahead, c), (x + ahead, c), (x + 2, c),
               (x, 1 - c), (x + ahead, 1 - c), (x - ahead, 1 - c), (x + 2, 1 - c))
    for t_ref, (xx, cc) in zip((t0, t1, t2, t3, t4, t5, t6, t7), sources):
        source = 2 * jnp.bitwise_and(xx + 4, 3) + cc
        tab_ref[:, pl.ds(pl.multiple_of(source * OWN, OWN), OWN), :] = t_ref[...]
    for j in range(NEL, JPAD):
        v_s[pl.ds(j, NBLK, stride=JPAD), :] = jnp.zeros((NBLK, GROUP), F32)
    x_s[...] = jnp.zeros_like(x_s)
    pick_a = oa_ref[...]

    def over_rows(jp, _):
        t = tab_ref[jp]
        x_s[...] += dot(chi_ref[jp], t, NT) + dot(clo_ref[jp], t, NT)
        for j2 in range(2):
            v_s[pl.ds(2 * jp + j2, NBLK, stride=JPAD), :] = dot(pick_a, t[:, j2 * V:(j2 + 1) * V], NT)
        return _

    lax.fori_loop(0, JP, over_rows, 0)

    def own_entry(blk, _):
        row = v_s[pl.ds(blk * JPAD + exc_smem[0, blk * BLOCK], 1), :]
        tia_ref[pl.ds(pl.multiple_of(blk * 8, 8), 8), :] = jnp.broadcast_to(row, (8, GROUP))
        return _

    lax.fori_loop(0, NBLK, own_entry, 0)
    acc_s[...] = jnp.zeros_like(acc_s)
    low = lax.broadcasted_iota(jnp.int32, (8, GROUP), 0) < STATES

    def pair(p, first):
        for h in range(2):
            blk = 2 * p + h
            dets = pl.ds(pl.multiple_of(blk * BLOCK, BLOCK), BLOCK)
            i = exc_smem[0, blk * BLOCK]
            t_i = tab_ref[lax.shift_right_logical(i, 1), :, pl.ds(pl.multiple_of(jnp.bitwise_and(i, 1) * V, V), V)]
            along = dot(obt_ref[dets, :], t_i, NT)
            column = v_s[pl.ds(pl.multiple_of(blk * JPAD, JPAD), JPAD), :].astype(BF16)
            down = dot(ojt_ref[dets, 0:JPAD], column)
            hi, lo = split(along * down)
            p_ref[dets, 0:GROUP] = hi
            p_ref[dets, GROUP:2 * GROUP] = lo
        both = pl.ds(pl.multiple_of(p * 2 * BLOCK, 2 * BLOCK), 2 * BLOCK)
        acc_s[...] += dot(c16_ref[:, both], p_ref[both, :])
        tia = jnp.where(low, tia_ref[pl.ds(pl.multiple_of(p * 16, 16), 8), :],
                        tia_ref[pl.ds(pl.multiple_of(p * 16 + 8, 8), 8), :])
        return first + x_s[pl.ds(pl.multiple_of(p * 8, 8), 8), :] * tia

    first = lax.fori_loop(0, PAIRS, pair, jnp.zeros((8, GROUP), F32))
    first = first + jnp.concatenate([first[STATES:], first[:STATES]], axis=0)
    second = acc_s[0:8, :] + acc_s[8:16, :]
    part_ref[...] = first - (second[:, 0:GROUP] + second[:, GROUP:2 * GROUP])


def grad_kernel(me_ref, p0, p1, p2, p3, energy_ref, exc_ref, tab_ref, p_ref, tia_ref, own_ref, out_ref, g_s, order_s):
    me = me_ref[1]
    for d, part in enumerate((p0, p1, p2, p3)):
        order_s[jnp.bitwise_and(lax.shift_right_logical(me, 1) - d + 4, 3)] = part[...]
    val = (order_s[0] + order_s[1]) + (order_s[2] + order_s[3])
    own = val[0:STATES, 0:OWN]
    for d in range(1, NDET):
        own = jnp.where(me == d, val[0:STATES, d * OWN:(d + 1) * OWN], own)
    own_ref[...] = own
    low = lax.broadcasted_iota(jnp.int32, (8, GROUP), 0) < STATES
    lane = lax.broadcasted_iota(jnp.int32, (8, GROUP), 1)
    square = val * val
    guide = 1.0 + jnp.sum(jnp.where(low, square, 0.0), axis=0, keepdims=True)
    energy = jnp.concatenate([energy_ref[...], energy_ref[...]], axis=0)
    middle = jnp.sum(energy, axis=1, keepdims=True) * (1.0 / GROUP)
    scaled = val / guide
    weight = square / guide
    sums = jnp.sum(jnp.where(low, weight, weight * energy), axis=1, keepdims=True)
    meta = jnp.where(lane == 0, sums, jnp.where(lane == 1, middle, 0.0))
    factor = jnp.where(low, scaled * (energy - middle), scaled)
    f_hi, f_lo = split(factor)
    f16 = jnp.concatenate([f_hi.astype(F32), f_lo.astype(F32)], axis=0).astype(BF16)
    f16 = jnp.concatenate([f16, f16], axis=1)
    lhs = tia_ref[...].reshape(NBLK, 8, GROUP) * factor[None]
    l_hi, l_lo = split(lhs.reshape(NBLK * 8, GROUP))
    lhs = jnp.concatenate([l_hi, l_lo], axis=1)

    def over_rows(jp, _):
        t = tab_ref[jp]
        g = dot(lhs, jnp.concatenate([t, t], axis=0)).reshape(NBLK, 8, 2 * V)
        hi, lo = split(jnp.concatenate([g[:, :, 0:V], g[:, :, V:2 * V]], axis=1))
        rows = pl.ds(pl.multiple_of(jp * 16, 16), 16)
        g_s[:, rows, 0:V] = hi
        g_s[:, rows, V:2 * V] = lo
        return _

    lax.fori_loop(0, JP, over_rows, 0)
    sub_b = lax.broadcasted_iota(jnp.int32, (V, BLOCK), 0)

    def slot(p, _):
        both = pl.ds(pl.multiple_of(p * 2 * BLOCK, 2 * BLOCK), 2 * BLOCK)
        second = dot(f16, p_ref[both, :], NT)
        second = second[0:8] + second[8:16]
        for h in range(2):
            dets = pl.ds(pl.multiple_of(p * 2 * BLOCK + h * BLOCK, BLOCK), BLOCK)
            j_row, b_row = exc_ref[2:3, dets], exc_ref[3:4, dets]
            pick_b = jnp.where(sub_b == b_row, 1.0, 0.0).astype(BF16)
            y = dot(g_s[2 * p + h], jnp.concatenate([pick_b, pick_b], axis=0))
            first = jnp.zeros((8, BLOCK), F32)
            for j in range(NEL):
                first = jnp.where(j_row == j, y[j * 8:(j + 1) * 8], first)
            out_ref[p, :, h * BLOCK:(h + 1) * BLOCK] = first - second[:, h * BLOCK:(h + 1) * BLOCK]
        out_ref[p, :, 2 * BLOCK:3 * BLOCK] = meta
        return _

    lax.fori_loop(0, NWALK, slot, 0)


def final_kernel(in_ref, grad_ref, energy_ref):
    meta = in_ref[0, :, 256:384]
    for g in range(1, NWALK):
        meta = meta + in_ref[g, :, 256:384]
    total, weighted = meta[0:STATES, 0:1], meta[STATES:8, 0:1]
    energy = weighted / total
    grad = jnp.zeros((STATES, 256), F32)
    for g in range(NWALK):
        shift = in_ref[g, 0:STATES, 257:258] - energy
        grad = grad + (in_ref[g, 0:STATES, 0:256] + shift * in_ref[g, STATES:8, 0:256])
    grad_ref[:, 0, :] = 2.0 * grad / total
    place = lax.broadcasted_iota(jnp.int32, (STATES, STATES), 0) == lax.broadcasted_iota(jnp.int32, (STATES, STATES), 1)
    energy_ref[...] = jnp.sum(jnp.where(place, energy, 0.0), axis=0, keepdims=True)


def params(mib):
    return pltpu.CompilerParams(vmem_limit_bytes=mib * MIB)


def make_table(positions, inverse, centers, exponent, orbital_weights):
    return pl.pallas_call(
        table_kernel,
        out_shape=jax.ShapeDtypeStruct((JP, OWN, 2 * V), BF16),
        in_specs=[pl.BlockSpec(memory_space=pltpu.HBM)] * 5, out_specs=vmem(1)[0],
        scratch_shapes=[pltpu.VMEM((3, OWN, NEL), F32), pltpu.VMEM((NEL, OWN, NEL), F32), pltpu.VMEM((3, NBAS), F32),
                        pltpu.VMEM((1, NBAS), F32), pltpu.VMEM((NBAS, V), F32), pltpu.VMEM((128, 128), F32), pltpu.VMEM((OWN * ROWS, NBAS), F32),
                        pltpu.VMEM((OWN, 128, V), F32), pltpu.VMEM((OWN, JPAD, 128), F32),
                        pltpu.VMEM((ROWS * OWN, V), F32), pltpu.SemaphoreType.DMA((5,))],
        compiler_params=params(8), name="tables",
    )(positions, inverse.transpose(1, 0, 2), centers, exponent.reshape(1, NBAS), orbital_weights)


def cost(flops):
    return pl.CostEstimate(flops=flops, bytes_accessed=8 * MIB, transcendentals=0)


def picks(excitations, coeffs):
    return pl.pallas_call(
        picks_kernel,
        out_shape=[jax.ShapeDtypeStruct((KD, V), BF16)] * 2
        + [jax.ShapeDtypeStruct((16, KD), BF16), jax.ShapeDtypeStruct((NBLK, V), BF16)],
        in_specs=[pl.BlockSpec(memory_space=pltpu.SMEM)] + vmem(2), out_specs=vmem(4),
        scratch_shapes=[pltpu.VMEM((NBLK, V), F32)],
        compiler_params=params(8), cost_estimate=cost(1_500_000_000), name="picks",
    )(excitations, excitations, coeffs)


def spread(excitations, coeffs):
    return pl.pallas_call(
        spread_kernel,
        out_shape=[jax.ShapeDtypeStruct((JP, NBLK * STATES, 2 * V), BF16)] * 2,
        in_specs=vmem(2), out_specs=vmem(2),
        compiler_params=params(8), cost_estimate=cost(1_500_000_000), name="spread",
    )(excitations, coeffs)


def partial_values(excitations, me, tables, spreads, picked):
    return pl.pallas_call(
        value_kernel,
        out_shape=[jax.ShapeDtypeStruct((8, GROUP), F32), jax.ShapeDtypeStruct((JP, GROUP, 2 * V), BF16),
                   jax.ShapeDtypeStruct((KD, 2 * GROUP), BF16), jax.ShapeDtypeStruct((NBLK * 8, GROUP), F32)],
        in_specs=[pl.BlockSpec(memory_space=pltpu.SMEM)] * 2 + vmem(NDET + 6), out_specs=vmem(4),
        scratch_shapes=[pltpu.VMEM((NBLK * JPAD, GROUP), F32), pltpu.VMEM((NBLK * STATES, GROUP), F32),
                        pltpu.VMEM((16, 2 * GROUP), F32)],
        compiler_params=params(22), name="partial_values",
    )(excitations, me, *tables, *spreads, *picked)


def gradient(me, parts, local_energy, excitations, tab, pair_products, tia):
    return pl.pallas_call(
        grad_kernel,
        out_shape=[jax.ShapeDtypeStruct((STATES, OWN), F32), jax.ShapeDtypeStruct((NWALK, 8, 384), F32)],
        in_specs=[pl.BlockSpec(memory_space=pltpu.SMEM)] + vmem(9), out_specs=vmem(2),
        scratch_shapes=[pltpu.VMEM((NBLK, JP * 16, 2 * V), BF16), pltpu.VMEM((4, 8, GROUP), F32)],
        compiler_params=params(20), name="gradient",
    )(me, *parts, local_energy, excitations, tab, pair_products, tia)


def finish(messages):
    return pl.pallas_call(
        final_kernel,
        out_shape=[jax.ShapeDtypeStruct((STATES, 1, 256), F32), jax.ShapeDtypeStruct((1, STATES), F32)],
        in_specs=vmem(1), out_specs=vmem(2),
        compiler_params=params(8), name="finish",
    )(messages)


def across(x, step):
    return lax.ppermute(x, "det", [(i, (i + 2 * step(i % 2)) % NDET) for i in range(NDET)])


def other_core(x):
    return lax.ppermute(x, "det", [(i, i ^ 1) for i in range(NDET)])


def gather_tables(table):
    ahead = across(table, lambda c: 1 - 2 * c)
    behind = across(table, lambda c: 2 * c - 1)
    beyond = across(ahead, lambda c: 1 - 2 * c)
    mine = [table, ahead, behind, beyond]
    return mine + [other_core(t) for t in mine]


def shards(positions, inverse, centers, exponent, orbital_weights, excitations, state_coeffs, local_energy):
    me = jnp.stack([lax.axis_index("walk"), lax.axis_index("det")])
    tables = gather_tables(make_table(positions, inverse, centers, exponent, orbital_weights))
    spreads = spread(excitations, state_coeffs)
    picked = picks(excitations, state_coeffs)
    part, tab, products, tia = partial_values(excitations, me, tables, spreads, picked)
    chip = part + other_core(part)
    parts = [chip] + [across(chip, lambda c, d=d: d) for d in (1, 2, 3)]
    own, messages = gradient(me, parts, local_energy, excitations, tab, products, tia)
    grad, energy = finish(lax.all_to_all(messages, "walk", 0, 0, tiled=True))
    return grad, own, energy.reshape(STATES)


def solution(mesh):
    in_specs = (
        P(None, ("walk", "det"), None),
        P(("walk", "det"), None, None),
        P(),
        P(),
        P(),
        P(None, "det"),
        P(None, "det"),
        P(None, "walk"),
    )
    out_specs = (P(None, "det", "walk"), P(None, ("walk", "det")), P())
    return jax.shard_map(shards, mesh=mesh, in_specs=in_specs, out_specs=out_specs, check_vma=False)
```

```python
import jax
import jax.numpy as jnp
from jax import lax
from jax.experimental import pallas as pl
from jax.experimental.pallas import tpu as pltpu
from jax.sharding import PartitionSpec as P

NEL = 50
ROWS = 56
V = 128
NBAS = 512
STATES = 4
BLOCK = 128
OWN = 16
GROUP = 128
KD = 8192
NBLK = KD // BLOCK
PAIRS = NBLK // 2
JP = NEL // 2
NDET = 8
NWALK = 32
JPAD = 64
MIB = 1024 * 1024
UNROLL = 8

F32, BF16 = jnp.float32, jnp.bfloat16
NN = (((1,), (0,)), ((), ()))
NT = (((1,), (1,)), ((), ()))
TN = (((0,), (0,)), ((), ()))


def dot(a, b, dims=NN):
    return lax.dot_general(a, b, dims, preferred_element_type=F32)


def split(x):
    hi = x.astype(BF16)
    return hi, (x - hi.astype(F32)).astype(BF16)


def vmem(n):
    return [pl.BlockSpec(memory_space=pltpu.VMEM)] * n


def table_kernel(pos_hbm, inv_hbm, cen_hbm, exp_hbm, orb_hbm, out_ref, pos_ref, inv_ref, cen_ref, exp_ref, orb_ref,
                 pos_s, basis_s, virt_s, inv_s, tab_s, sems):
    copies = [pltpu.make_async_copy(src, dst, sems.at[n]) for n, (src, dst) in enumerate(
        ((pos_hbm, pos_ref), (cen_hbm, cen_ref), (exp_hbm, exp_ref), (orb_hbm, orb_ref), (inv_hbm, inv_ref)))]
    for copy in copies:
        copy.start()
    pos_s[...] = jnp.zeros_like(pos_s)
    virt_s[...] = jnp.zeros_like(virt_s)
    inv_s[...] = jnp.zeros_like(inv_s)
    for copy in copies[:3]:
        copy.wait()
    for c in range(3):
        pos_s[c * OWN:(c + 1) * OWN, 0:NEL] = pos_ref[c]
    cols = pos_s[...].T
    neg = -exp_ref[...]
    for w in range(OWN):
        dist = jnp.zeros((ROWS, NBAS), F32)
        for c in range(3):
            off = cols[0:ROWS, c * OWN + w:c * OWN + w + 1] - cen_ref[c:c + 1, :]
            dist = dist + off * off
        basis_s[w * ROWS:(w + 1) * ROWS, :] = jnp.exp(neg * dist)
    b_hi, b_lo = split(basis_s[...])
    copies[3].wait()
    o_hi, o_lo = split(orb_ref[...])
    virt = dot(b_hi, o_hi) + (dot(b_hi, o_lo) + dot(b_lo, o_hi))
    for w in range(OWN):
        virt_s[w, 0:ROWS, :] = virt[w * ROWS:(w + 1) * ROWS]
    copies[4].wait()
    for w in range(OWN):
        inv_s[w, 0:NEL, 0:NEL] = inv_ref[:, w, :]
    for w in range(OWN):
        i_hi, i_lo = split(inv_s[w])
        v_hi, v_lo = split(virt_s[w])
        table = dot(i_hi, v_hi) + (dot(i_hi, v_lo) + dot(i_lo, v_hi))
        tab_s[pl.ds(w, ROWS, stride=OWN), :] = table[0:ROWS]
    for i in range(NEL):
        out_ref[:, i * V:(i + 1) * V] = tab_s[i * OWN:(i + 1) * OWN, :].astype(BF16)


def spread_kernel(exc_ref, coef_ref, spread_ref):
    sub_b = lax.broadcasted_iota(jnp.int32, (V, 2 * BLOCK), 0)
    half = lax.broadcasted_iota(jnp.int32, (8, 2 * BLOCK), 1) // BLOCK
    upper = lax.broadcasted_iota(jnp.int32, (8, 2 * BLOCK), 0) // STATES

    def quad(q, _):
        parts = []
        for h in range(2):
            where = pl.ds(pl.multiple_of((2 * q + h) * 2 * BLOCK, 2 * BLOCK), 2 * BLOCK)
            j_row, b_row = exc_ref[2:3, where], exc_ref[3:4, where]
            c4 = coef_ref[:, where]
            c_hi, c_lo = split(jnp.concatenate([c4, c4], axis=0))
            own = half == upper
            q_hi = jnp.where(own, c_hi.astype(F32), 0.0)
            q_lo = jnp.where(own, c_lo.astype(F32), 0.0)
            pick_b = jnp.where(sub_b == b_row, 1.0, 0.0).astype(BF16)
            w_hi, w_lo = [], []
            for jp in range(JP):
                m0, m1 = j_row == 2 * jp, j_row == 2 * jp + 1
                w_hi.append(jnp.concatenate([jnp.where(m0, q_hi, 0.0), jnp.where(m1, q_hi, 0.0)], axis=0).astype(BF16))
                w_lo.append(jnp.concatenate([jnp.where(m0, q_lo, 0.0), jnp.where(m1, q_lo, 0.0)], axis=0).astype(BF16))
            parts.append(dot(jnp.concatenate(w_hi, axis=0), pick_b, NT) + dot(jnp.concatenate(w_lo, axis=0), pick_b, NT))
        high = pl.ds(pl.multiple_of(q * 16, 16), 16)
        low = pl.ds(pl.multiple_of(NBLK * STATES + q * 16, 16), 16)
        for j in range(NEL):
            both = jnp.concatenate([parts[0][j * 8:(j + 1) * 8], parts[1][j * 8:(j + 1) * 8]], axis=0)
            hi, lo = split(both)
            spread_ref[high, j * V:(j + 1) * V] = hi
            spread_ref[low, j * V:(j + 1) * V] = lo
        return _

    lax.fori_loop(0, PAIRS // 2, quad, 0)


def value_kernel(par_ref, me_ref, t0, t1, t2, t3, t4, t5, t6, t7, spread_ref, exc_ref, coef_ref,
                 part_ref, tab_ref, p_ref, tia_ref, v_s, x_s, oa_s, acc_s):
    x, c = lax.shift_right_logical(me_ref[1], 1), jnp.bitwise_and(me_ref[1], 1)
    ahead = 1 - 2 * c
    sources = ((x, c), (x - ahead, c), (x + ahead, c), (x + 2, c),
               (x, 1 - c), (x + ahead, 1 - c), (x - ahead, 1 - c), (x + 2, 1 - c))
    for t_ref, (xx, cc) in zip((t0, t1, t2, t3, t4, t5, t6, t7), sources):
        source = 2 * jnp.bitwise_and(xx + 4, 3) + cc
        tab_ref[pl.ds(pl.multiple_of(source * OWN, OWN), OWN), :] = t_ref[...]
    for j in range(NEL, JPAD):
        v_s[pl.ds(j, NBLK, stride=JPAD), :] = jnp.zeros((NBLK, GROUP), F32)
    lane = lax.broadcasted_iota(jnp.int32, (1, V), 1)
    for blk in range(NBLK):
        oa_s[blk:blk + 1, :] = jnp.where(lane == par_ref[1, blk], 1.0, 0.0).astype(F32)
    pick_a = oa_s[...].astype(BF16)
    x = dot(spread_ref[...], tab_ref[...], NT)
    x_s[...] = x[0:NBLK * STATES] + x[NBLK * STATES:]
    for j in range(NEL):
        v_s[pl.ds(j, NBLK, stride=JPAD), :] = dot(pick_a, tab_ref[:, j * V:(j + 1) * V], NT)

    def own_entry(blk, _):
        row = v_s[pl.ds(blk * JPAD + par_ref[0, blk], 1), :]
        tia_ref[pl.ds(pl.multiple_of(blk * 8, 8), 8), :] = jnp.broadcast_to(row, (8, GROUP))
        return _

    lax.fori_loop(0, NBLK, own_entry, 0, unroll=8)
    acc_s[...] = jnp.zeros_like(acc_s)
    low = lax.broadcasted_iota(jnp.int32, (8, GROUP), 0) < STATES
    sub_b = lax.broadcasted_iota(jnp.int32, (V, BLOCK), 0)
    sub_j = lax.broadcasted_iota(jnp.int32, (JPAD, BLOCK), 0)

    def pair(p, first):
        products = []
        for h in range(2):
            blk = 2 * p + h
            dets = pl.ds(pl.multiple_of(blk * BLOCK, BLOCK), BLOCK)
            pick_j = jnp.where(sub_j == exc_ref[2:3, dets], 1.0, 0.0).astype(BF16)
            pick_b = jnp.where(sub_b == exc_ref[3:4, dets], 1.0, 0.0).astype(BF16)
            t_i = tab_ref[:, pl.ds(pl.multiple_of(par_ref[0, blk] * V, V), V)]
            along = dot(t_i, pick_b)
            column = v_s[pl.ds(pl.multiple_of(blk * JPAD, JPAD), JPAD), :].astype(BF16)
            down = dot(column, pick_j, TN)
            product = along * down
            hi, lo = split(product)
            p_ref[0:GROUP, dets] = hi
            p_ref[GROUP:2 * GROUP, dets] = lo
            products.append((product, dets))
        for s in range(STATES):
            acc_s[s] += products[0][0] * coef_ref[s:s + 1, products[0][1]] + products[1][0] * coef_ref[s:s + 1, products[1][1]]
        tia = jnp.where(low, tia_ref[pl.ds(pl.multiple_of(p * 16, 16), 8), :],
                        tia_ref[pl.ds(pl.multiple_of(p * 16 + 8, 8), 8), :])
        return first + x_s[pl.ds(pl.multiple_of(p * 8, 8), 8), :] * tia

    first = lax.fori_loop(0, PAIRS, pair, jnp.zeros((8, GROUP), F32), unroll=UNROLL)
    first = first + jnp.concatenate([first[STATES:], first[:STATES]], axis=0)
    second = jnp.concatenate([jnp.sum(acc_s[s].T, axis=0, keepdims=True) for s in range(STATES)] * 2, axis=0)
    part_ref[...] = first - second


def grad_kernel(me_ref, p0, p1, p2, p3, energy_ref, exc_ref, tab_ref, p_ref, tia_ref, own_ref, out_ref, g_s, order_s):
    me = me_ref[1]
    for d, part in enumerate((p0, p1, p2, p3)):
        order_s[jnp.bitwise_and(lax.shift_right_logical(me, 1) - d + 4, 3)] = part[...]
    val = (order_s[0] + order_s[1]) + (order_s[2] + order_s[3])
    own = val[0:STATES, 0:OWN]
    for d in range(1, NDET):
        own = jnp.where(me == d, val[0:STATES, d * OWN:(d + 1) * OWN], own)
    own_ref[...] = own
    low = lax.broadcasted_iota(jnp.int32, (8, GROUP), 0) < STATES
    lane = lax.broadcasted_iota(jnp.int32, (8, GROUP), 1)
    square = val * val
    guide = 1.0 + jnp.sum(jnp.where(low, square, 0.0), axis=0, keepdims=True)
    energy = jnp.concatenate([energy_ref[...], energy_ref[...]], axis=0)
    middle = jnp.sum(energy, axis=1, keepdims=True) * (1.0 / GROUP)
    scaled = val / guide
    weight = square / guide
    sums = jnp.sum(jnp.where(low, weight, weight * energy), axis=1, keepdims=True)
    meta = jnp.where(lane == 0, sums, jnp.where(lane == 1, middle, 0.0))
    factor = jnp.where(low, scaled * (energy - middle), scaled)
    f_hi, f_lo = split(factor)
    f16 = jnp.concatenate([f_hi.astype(F32), f_lo.astype(F32)], axis=0).astype(BF16)
    f16 = jnp.concatenate([f16, f16], axis=1)
    lhs = tia_ref[...].reshape(NBLK, 8, GROUP) * factor[None]
    l_hi, l_lo = split(lhs.reshape(NBLK * 8, GROUP))
    lhs = jnp.concatenate([l_hi, l_lo], axis=1)

    for jp in range(JP):
        t = tab_ref[:, jp * 2 * V:(jp + 1) * 2 * V]
        g = dot(lhs, jnp.concatenate([t, t], axis=0)).reshape(NBLK, 8, 2 * V)
        hi, lo = split(jnp.concatenate([g[:, :, 0:V], g[:, :, V:2 * V]], axis=1))
        g_s[:, jp * 16:(jp + 1) * 16, 0:V] = hi
        g_s[:, jp * 16:(jp + 1) * 16, V:2 * V] = lo
    sub_b = lax.broadcasted_iota(jnp.int32, (V, BLOCK), 0)

    def slot(p, _):
        both = pl.ds(pl.multiple_of(p * 2 * BLOCK, 2 * BLOCK), 2 * BLOCK)
        second = dot(f16, p_ref[:, both])
        second = second[0:8] + second[8:16]
        for h in range(2):
            dets = pl.ds(pl.multiple_of(p * 2 * BLOCK + h * BLOCK, BLOCK), BLOCK)
            j_row, b_row = exc_ref[2:3, dets], exc_ref[3:4, dets]
            pick_b = jnp.where(sub_b == b_row, 1.0, 0.0).astype(BF16)
            y = dot(g_s[2 * p + h], jnp.concatenate([pick_b, pick_b], axis=0))
            first = jnp.zeros((8, BLOCK), F32)
            for j in range(NEL):
                first = jnp.where(j_row == j, y[j * 8:(j + 1) * 8], first)
            out_ref[p, :, h * BLOCK:(h + 1) * BLOCK] = first - second[:, h * BLOCK:(h + 1) * BLOCK]
        out_ref[p, :, 2 * BLOCK:3 * BLOCK] = meta
        return _

    lax.fori_loop(0, NWALK, slot, 0, unroll=UNROLL)


def final_kernel(in_ref, grad_ref, energy_ref):
    meta = in_ref[0, :, 256:384]
    for g in range(1, NWALK):
        meta = meta + in_ref[g, :, 256:384]
    total, weighted = meta[0:STATES, 0:1], meta[STATES:8, 0:1]
    energy = weighted / total
    grad = jnp.zeros((STATES, 256), F32)
    for g in range(NWALK):
        shift = in_ref[g, 0:STATES, 257:258] - energy
        grad = grad + (in_ref[g, 0:STATES, 0:256] + shift * in_ref[g, STATES:8, 0:256])
    grad_ref[:, 0, :] = 2.0 * grad / total
    place = lax.broadcasted_iota(jnp.int32, (STATES, STATES), 0) == lax.broadcasted_iota(jnp.int32, (STATES, STATES), 1)
    energy_ref[...] = jnp.sum(jnp.where(place, energy, 0.0), axis=0, keepdims=True)


def params(mib):
    return pltpu.CompilerParams(vmem_limit_bytes=mib * MIB)


def make_table(positions, inverse, centers, exponent, orbital_weights):
    return pl.pallas_call(
        table_kernel,
        out_shape=jax.ShapeDtypeStruct((OWN, NEL * V), BF16),
        in_specs=[pl.BlockSpec(memory_space=pltpu.HBM)] * 5, out_specs=vmem(1)[0],
        scratch_shapes=[pltpu.VMEM((3, OWN, NEL), F32), pltpu.VMEM((NEL, OWN, NEL), F32), pltpu.VMEM((3, NBAS), F32),
                        pltpu.VMEM((1, NBAS), F32), pltpu.VMEM((NBAS, V), F32), pltpu.VMEM((128, 128), F32), pltpu.VMEM((OWN * ROWS, NBAS), F32),
                        pltpu.VMEM((OWN, 128, V), F32), pltpu.VMEM((OWN, JPAD, 128), F32),
                        pltpu.VMEM((ROWS * OWN, V), F32), pltpu.SemaphoreType.DMA((5,))],
        compiler_params=params(60), name="tables",
    )(positions, inverse.transpose(1, 0, 2), centers, exponent.reshape(1, NBAS), orbital_weights)


def cost(flops):
    return pl.CostEstimate(flops=flops, bytes_accessed=8 * MIB, transcendentals=0)


def spread(excitations, coeffs):
    return pl.pallas_call(
        spread_kernel,
        out_shape=jax.ShapeDtypeStruct((2 * NBLK * STATES, NEL * V), BF16),
        in_specs=vmem(2), out_specs=vmem(1)[0],
        compiler_params=params(8), cost_estimate=cost(1_500_000_000), name="spread",
    )(excitations, coeffs)


def partial_values(parents, me, tables, spreads, excitations, coeffs):
    return pl.pallas_call(
        value_kernel,
        out_shape=[jax.ShapeDtypeStruct((8, GROUP), F32), jax.ShapeDtypeStruct((GROUP, NEL * V), BF16),
                   jax.ShapeDtypeStruct((2 * GROUP, KD), BF16), jax.ShapeDtypeStruct((NBLK * 8, GROUP), F32)],
        in_specs=[pl.BlockSpec(memory_space=pltpu.SMEM)] * 2 + vmem(NDET + 3), out_specs=vmem(4),
        scratch_shapes=[pltpu.VMEM((NBLK * JPAD, GROUP), F32), pltpu.VMEM((NBLK * STATES, GROUP), F32),
                        pltpu.VMEM((NBLK, V), F32), pltpu.VMEM((STATES, GROUP, BLOCK), F32)],
        compiler_params=params(22), name="partial_values",
    )(parents, me, *tables, spreads, excitations, coeffs)


def gradient(me, parts, local_energy, excitations, tab, pair_products, tia):
    return pl.pallas_call(
        grad_kernel,
        out_shape=[jax.ShapeDtypeStruct((STATES, OWN), F32), jax.ShapeDtypeStruct((NWALK, 8, 384), F32)],
        in_specs=[pl.BlockSpec(memory_space=pltpu.SMEM)] + vmem(9), out_specs=vmem(2),
        scratch_shapes=[pltpu.VMEM((NBLK, JP * 16, 2 * V), BF16), pltpu.VMEM((4, 8, GROUP), F32)],
        compiler_params=params(20), name="gradient",
    )(me, *parts, local_energy, excitations, tab, pair_products, tia)


def finish(messages):
    return pl.pallas_call(
        final_kernel,
        out_shape=[jax.ShapeDtypeStruct((STATES, 1, 256), F32), jax.ShapeDtypeStruct((1, STATES), F32)],
        in_specs=vmem(1), out_specs=vmem(2),
        compiler_params=params(8), name="finish",
    )(messages)


def across(x, step):
    return lax.ppermute(x, "det", [(i, (i + 2 * step(i % 2)) % NDET) for i in range(NDET)])


def other_core(x):
    return lax.ppermute(x, "det", [(i, i ^ 1) for i in range(NDET)])


def gather_tables(table):
    ahead = across(table, lambda c: 1 - 2 * c)
    behind = across(table, lambda c: 2 * c - 1)
    beyond = across(ahead, lambda c: 1 - 2 * c)
    mine = [table, ahead, behind, beyond]
    return mine + [other_core(t) for t in mine]


def shards(positions, inverse, centers, exponent, orbital_weights, excitations, state_coeffs, local_energy):
    me = jnp.stack([lax.axis_index("walk"), lax.axis_index("det")])
    table = make_table(positions, inverse, centers, exponent, orbital_weights)
    tables = gather_tables(table)
    spreads = spread(excitations, state_coeffs)
    parents = excitations[0:2, ::BLOCK]
    part, tab, products, tia = partial_values(parents, me, tables, spreads, excitations, state_coeffs)
    chip = part + other_core(part)
    parts = [chip] + [across(chip, lambda c, d=d: d) for d in (1, 2, 3)]
    own, messages = gradient(me, parts, local_energy, excitations, tab, products, tia)
    grad, energy = finish(lax.all_to_all(messages, "walk", 0, 0, tiled=True))
    return grad, own, energy.reshape(STATES)


def solution(mesh):
    in_specs = (
        P(None, ("walk", "det"), None),
        P(("walk", "det"), None, None),
        P(),
        P(),
        P(),
        P(None, "det"),
        P(None, "det"),
        P(None, "walk"),
    )
    out_specs = (P(None, "det", "walk"), P(None, ("walk", "det")), P())
    return jax.shard_map(shards, mesh=mesh, in_specs=in_specs, out_specs=out_specs, check_vma=False)
```

```python
import functools

import jax
import jax.numpy as jnp
from jax import lax
from jax.experimental import pallas as pl
from jax.experimental.pallas import tpu as pltpu
from jax.sharding import PartitionSpec as P

NEL = 50
ROWS = 56
V = 128
NBAS = 512
STATES = 4
BLOCK = 128
OWN = 16
GROUP = 128
KD = 8192
NBLK = KD // BLOCK
PAIRS = NBLK // 2
JP = NEL // 2
NDET = 8
NWALK = 32
JPAD = 64
MIB = 1024 * 1024
UNROLL = 8
QUADS = PAIRS // 4

F32, BF16 = jnp.float32, jnp.bfloat16
NN = (((1,), (0,)), ((), ()))
NT = (((1,), (1,)), ((), ()))
TN = (((0,), (0,)), ((), ()))


def dot(a, b, dims=NN):
    return lax.dot_general(a, b, dims, preferred_element_type=F32)


def split(x):
    hi = x.astype(BF16)
    return hi, (x - hi.astype(F32)).astype(BF16)


def vmem(n):
    return [pl.BlockSpec(memory_space=pltpu.VMEM)] * n


def table_kernel(pos_hbm, inv_hbm, cen_hbm, exp_hbm, orb_hbm, out_ref, pos_ref, inv_ref, cen_ref, exp_ref, orb_ref,
                 pos_s, basis_s, virt_s, inv_s, tab_s, sems):
    copies = [pltpu.make_async_copy(src, dst, sems.at[n]) for n, (src, dst) in enumerate(
        ((pos_hbm, pos_ref), (cen_hbm, cen_ref), (exp_hbm, exp_ref), (orb_hbm, orb_ref), (inv_hbm, inv_ref)))]
    for copy in copies:
        copy.start()
    pos_s[...] = jnp.zeros_like(pos_s)
    virt_s[...] = jnp.zeros_like(virt_s)
    inv_s[...] = jnp.zeros_like(inv_s)
    for copy in copies[:3]:
        copy.wait()
    for c in range(3):
        pos_s[c * OWN:(c + 1) * OWN, 0:NEL] = pos_ref[c]
    cols = pos_s[...].T
    neg = -exp_ref[...]
    for w in range(OWN):
        dist = jnp.zeros((ROWS, NBAS), F32)
        for c in range(3):
            off = cols[0:ROWS, c * OWN + w:c * OWN + w + 1] - cen_ref[c:c + 1, :]
            dist = dist + off * off
        basis_s[w * ROWS:(w + 1) * ROWS, :] = jnp.exp(neg * dist)
    b_hi, b_lo = split(basis_s[...])
    copies[3].wait()
    o_hi, o_lo = split(orb_ref[...])
    virt = dot(b_hi, o_hi) + (dot(b_hi, o_lo) + dot(b_lo, o_hi))
    for w in range(OWN):
        virt_s[w, 0:ROWS, :] = virt[w * ROWS:(w + 1) * ROWS]
    copies[4].wait()
    for w in range(OWN):
        inv_s[w, 0:NEL, 0:NEL] = inv_ref[:, w, :]
    for w in range(OWN):
        i_hi, i_lo = split(inv_s[w])
        v_hi, v_lo = split(virt_s[w])
        table = dot(i_hi, v_hi) + (dot(i_hi, v_lo) + dot(i_lo, v_hi))
        tab_s[pl.ds(w, ROWS, stride=OWN), :] = table[0:ROWS]
    for i in range(NEL):
        out_ref[:, i * V:(i + 1) * V] = tab_s[i * OWN:(i + 1) * OWN, :].astype(BF16)


def columns_kernel(par_ref, exc_ref, coef_ref, spread_ref, oa_ref, oa_s):
    lane = lax.broadcasted_iota(jnp.int32, (1, V), 1)
    for blk in range(NBLK):
        oa_s[blk:blk + 1, :] = jnp.where(lane == par_ref[1, blk], 1.0, 0.0).astype(F32)
    oa_ref[...] = oa_s[...].astype(BF16)
    spread_kernel(0, exc_ref, coef_ref, spread_ref)


def spread_kernel(side, exc_ref, coef_ref, spread_ref):
    sub_b = lax.broadcasted_iota(jnp.int32, (V, 2 * BLOCK), 0)
    half = lax.broadcasted_iota(jnp.int32, (8, 2 * BLOCK), 1) // BLOCK
    upper = lax.broadcasted_iota(jnp.int32, (8, 2 * BLOCK), 0) // STATES

    def quad(q, _):
        parts = []
        for h in range(2):
            where = pl.ds(pl.multiple_of((side * QUADS * 2 + 2 * q + h) * 2 * BLOCK, 2 * BLOCK), 2 * BLOCK)
            j_row, b_row = exc_ref[2:3, where], exc_ref[3:4, where]
            c4 = coef_ref[:, where]
            c_hi, c_lo = split(jnp.concatenate([c4, c4], axis=0))
            own = half == upper
            q_hi = jnp.where(own, c_hi.astype(F32), 0.0)
            q_lo = jnp.where(own, c_lo.astype(F32), 0.0)
            pick_b = jnp.where(sub_b == b_row, 1.0, 0.0).astype(BF16)
            w_hi, w_lo = [], []
            for jp in range(JP):
                m0, m1 = j_row == 2 * jp, j_row == 2 * jp + 1
                w_hi.append(jnp.concatenate([jnp.where(m0, q_hi, 0.0), jnp.where(m1, q_hi, 0.0)], axis=0).astype(BF16))
                w_lo.append(jnp.concatenate([jnp.where(m0, q_lo, 0.0), jnp.where(m1, q_lo, 0.0)], axis=0).astype(BF16))
            parts.append(dot(jnp.concatenate(w_hi, axis=0), pick_b, NT) + dot(jnp.concatenate(w_lo, axis=0), pick_b, NT))
        high = pl.ds(pl.multiple_of(q * 16, 16), 16)
        low = pl.ds(pl.multiple_of(QUADS * 16 + q * 16, 16), 16)
        for j in range(NEL):
            both = jnp.concatenate([parts[0][j * 8:(j + 1) * 8], parts[1][j * 8:(j + 1) * 8]], axis=0)
            hi, lo = split(both)
            spread_ref[high, j * V:(j + 1) * V] = hi
            spread_ref[low, j * V:(j + 1) * V] = lo
        return _

    lax.fori_loop(0, QUADS, quad, 0)


def value_kernel(par_ref, me_ref, t0, t1, t2, t3, t4, t5, t6, t7, half0, half1, oa_ref, exc_ref, coef_ref,
                 part_ref, tab_ref, p_ref, tia_ref, v_s, x_s, acc_s):
    x, c = lax.shift_right_logical(me_ref[1], 1), jnp.bitwise_and(me_ref[1], 1)
    ahead = 1 - 2 * c
    sources = ((x, c), (x - ahead, c), (x + ahead, c), (x + 2, c),
               (x, 1 - c), (x + ahead, 1 - c), (x - ahead, 1 - c), (x + 2, 1 - c))
    for t_ref, (xx, cc) in zip((t0, t1, t2, t3, t4, t5, t6, t7), sources):
        source = 2 * jnp.bitwise_and(xx + 4, 3) + cc
        tab_ref[pl.ds(pl.multiple_of(source * OWN, OWN), OWN), :] = t_ref[...]
    for j in range(NEL, JPAD):
        v_s[pl.ds(j, NBLK, stride=JPAD), :] = jnp.zeros((NBLK, GROUP), F32)
    rows = QUADS * 16
    for side, half in enumerate((half0, half1)):
        x = dot(half[...], tab_ref[...], NT)
        x_s[side * rows:(side + 1) * rows, :] = x[0:rows] + x[rows:]
    pick_a = oa_ref[...]
    for j in range(NEL):
        v_s[pl.ds(j, NBLK, stride=JPAD), :] = dot(pick_a, tab_ref[:, j * V:(j + 1) * V], NT)

    def own_entry(blk, _):
        row = v_s[pl.ds(blk * JPAD + par_ref[0, blk], 1), :]
        tia_ref[pl.ds(pl.multiple_of(blk * 8, 8), 8), :] = jnp.broadcast_to(row, (8, GROUP))
        return _

    lax.fori_loop(0, NBLK, own_entry, 0, unroll=8)
    acc_s[...] = jnp.zeros_like(acc_s)
    low = lax.broadcasted_iota(jnp.int32, (8, GROUP), 0) < STATES
    sub_b = lax.broadcasted_iota(jnp.int32, (V, BLOCK), 0)
    sub_j = lax.broadcasted_iota(jnp.int32, (JPAD, BLOCK), 0)

    def pair(p, first):
        products = []
        for h in range(2):
            blk = 2 * p + h
            dets = pl.ds(pl.multiple_of(blk * BLOCK, BLOCK), BLOCK)
            pick_j = jnp.where(sub_j == exc_ref[2:3, dets], 1.0, 0.0).astype(BF16)
            pick_b = jnp.where(sub_b == exc_ref[3:4, dets], 1.0, 0.0).astype(BF16)
            t_i = tab_ref[:, pl.ds(pl.multiple_of(par_ref[0, blk] * V, V), V)]
            along = dot(t_i, pick_b)
            column = v_s[pl.ds(pl.multiple_of(blk * JPAD, JPAD), JPAD), :].astype(BF16)
            down = dot(column, pick_j, TN)
            product = along * down
            hi, lo = split(product)
            p_ref[0:GROUP, dets] = hi
            p_ref[GROUP:2 * GROUP, dets] = lo
            products.append((product, dets))
        for s in range(STATES):
            acc_s[s] += products[0][0] * coef_ref[s:s + 1, products[0][1]] + products[1][0] * coef_ref[s:s + 1, products[1][1]]
        tia = jnp.where(low, tia_ref[pl.ds(pl.multiple_of(p * 16, 16), 8), :],
                        tia_ref[pl.ds(pl.multiple_of(p * 16 + 8, 8), 8), :])
        return first + x_s[pl.ds(pl.multiple_of(p * 8, 8), 8), :] * tia

    first = lax.fori_loop(0, PAIRS, pair, jnp.zeros((8, GROUP), F32), unroll=UNROLL)
    first = first + jnp.concatenate([first[STATES:], first[:STATES]], axis=0)
    second = jnp.concatenate([jnp.sum(acc_s[s].T, axis=0, keepdims=True) for s in range(STATES)] * 2, axis=0)
    part_ref[...] = first - second


def grad_kernel(me_ref, p0, p1, p2, p3, energy_ref, exc_ref, tab_ref, p_ref, tia_ref, own_ref, out_ref, g_s, order_s):
    me = me_ref[1]
    for d, part in enumerate((p0, p1, p2, p3)):
        order_s[jnp.bitwise_and(lax.shift_right_logical(me, 1) - d + 4, 3)] = part[...]
    val = (order_s[0] + order_s[1]) + (order_s[2] + order_s[3])
    own = val[0:STATES, 0:OWN]
    for d in range(1, NDET):
        own = jnp.where(me == d, val[0:STATES, d * OWN:(d + 1) * OWN], own)
    own_ref[...] = own
    low = lax.broadcasted_iota(jnp.int32, (8, GROUP), 0) < STATES
    lane = lax.broadcasted_iota(jnp.int32, (8, GROUP), 1)
    square = val * val
    guide = 1.0 + jnp.sum(jnp.where(low, square, 0.0), axis=0, keepdims=True)
    energy = jnp.concatenate([energy_ref[...], energy_ref[...]], axis=0)
    middle = jnp.sum(energy, axis=1, keepdims=True) * (1.0 / GROUP)
    scaled = val / guide
    weight = square / guide
    sums = jnp.sum(jnp.where(low, weight, weight * energy), axis=1, keepdims=True)
    meta = jnp.zeros((8, GROUP), F32)
    for at, value in ((0, sums), (3, middle)):
        for n in range(3):
            piece = value.astype(BF16).astype(F32)
            meta = jnp.where(lane == at + n, piece, meta)
            value = value - piece
    meta = jnp.concatenate([meta, meta], axis=0).astype(BF16)
    factor = jnp.where(low, scaled * (energy - middle), scaled)
    f_hi, f_lo = split(factor)
    f16 = jnp.concatenate([f_hi.astype(F32), f_lo.astype(F32)], axis=0).astype(BF16)
    f16 = jnp.concatenate([f16, f16], axis=1)
    lhs = tia_ref[...].reshape(NBLK, 8, GROUP) * factor[None]
    l_hi, l_lo = split(lhs.reshape(NBLK * 8, GROUP))
    lhs = jnp.concatenate([l_hi, l_lo], axis=1)

    for jp in range(JP):
        t = tab_ref[:, jp * 2 * V:(jp + 1) * 2 * V]
        g = dot(lhs, jnp.concatenate([t, t], axis=0)).reshape(NBLK, 8, 2 * V)
        hi, lo = split(jnp.concatenate([g[:, :, 0:V], g[:, :, V:2 * V]], axis=1))
        g_s[:, jp * 16:(jp + 1) * 16, 0:V] = hi
        g_s[:, jp * 16:(jp + 1) * 16, V:2 * V] = lo
    sub_b = lax.broadcasted_iota(jnp.int32, (V, BLOCK), 0)

    def slot(p, _):
        both = pl.ds(pl.multiple_of(p * 2 * BLOCK, 2 * BLOCK), 2 * BLOCK)
        second = dot(f16, p_ref[:, both])
        second = second[0:8] + second[8:16]
        terms = []
        for h in range(2):
            dets = pl.ds(pl.multiple_of(p * 2 * BLOCK + h * BLOCK, BLOCK), BLOCK)
            j_row, b_row = exc_ref[2:3, dets], exc_ref[3:4, dets]
            pick_b = jnp.where(sub_b == b_row, 1.0, 0.0).astype(BF16)
            y = dot(g_s[2 * p + h], jnp.concatenate([pick_b, pick_b], axis=0))
            first = jnp.zeros((8, BLOCK), F32)
            for j in range(NEL):
                first = jnp.where(j_row == j, y[j * 8:(j + 1) * 8], first)
            terms.append(first - second[:, h * BLOCK:(h + 1) * BLOCK])
        out_ref[p, :, 0:BLOCK] = jnp.concatenate(terms, axis=0).astype(BF16)
        out_ref[p, :, BLOCK:2 * BLOCK] = meta
        return _

    lax.fori_loop(0, NWALK, slot, 0, unroll=UNROLL)


def final_kernel(in_ref, grad_ref, energy_ref):
    lane = lax.broadcasted_iota(jnp.int32, (8, BLOCK), 1)
    metas = [in_ref[g].astype(F32)[0:8, BLOCK:2 * BLOCK] for g in range(NWALK)]
    meta = metas[0]
    for g in range(1, NWALK):
        meta = meta + metas[g]
    sums = jnp.sum(jnp.where(lane < 3, meta, 0.0), axis=1, keepdims=True)
    total, weighted = sums[0:STATES], sums[STATES:8]
    energy = weighted / total
    grads = [jnp.zeros((STATES, BLOCK), F32)] * 2
    for g in range(NWALK):
        terms = in_ref[g].astype(F32)
        middle = jnp.sum(jnp.where((lane >= 3) & (lane < 6), metas[g], 0.0), axis=1, keepdims=True)
        shift = middle[0:STATES] - energy
        for h in range(2):
            grads[h] = grads[h] + (terms[h * 8:h * 8 + STATES, 0:BLOCK]
                                   + shift * terms[h * 8 + STATES:h * 8 + 8, 0:BLOCK])
    scale = 2.0 / total
    grad_ref[:, 0, 0:BLOCK] = grads[0] * scale
    grad_ref[:, 0, BLOCK:2 * BLOCK] = grads[1] * scale
    place = lax.broadcasted_iota(jnp.int32, (STATES, STATES), 0) == lax.broadcasted_iota(jnp.int32, (STATES, STATES), 1)
    energy_ref[...] = jnp.sum(jnp.where(place, energy, 0.0), axis=0, keepdims=True)


def params(mib):
    return pltpu.CompilerParams(vmem_limit_bytes=mib * MIB)


def make_table(positions, inverse, centers, exponent, orbital_weights):
    return pl.pallas_call(
        table_kernel,
        out_shape=jax.ShapeDtypeStruct((OWN, NEL * V), BF16),
        in_specs=[pl.BlockSpec(memory_space=pltpu.HBM)] * 5, out_specs=vmem(1)[0],
        scratch_shapes=[pltpu.VMEM((3, OWN, NEL), F32), pltpu.VMEM((NEL, OWN, NEL), F32), pltpu.VMEM((3, NBAS), F32),
                        pltpu.VMEM((1, NBAS), F32), pltpu.VMEM((NBAS, V), F32), pltpu.VMEM((128, 128), F32), pltpu.VMEM((OWN * ROWS, NBAS), F32),
                        pltpu.VMEM((OWN, 128, V), F32), pltpu.VMEM((OWN, JPAD, 128), F32),
                        pltpu.VMEM((ROWS * OWN, V), F32), pltpu.SemaphoreType.DMA((5,))],
        compiler_params=params(60), name="tables",
    )(positions, inverse.transpose(1, 0, 2), centers, exponent.reshape(1, NBAS), orbital_weights)


def cost(flops):
    return pl.CostEstimate(flops=flops, bytes_accessed=8 * MIB, transcendentals=0)


def spread_first(parents, excitations, coeffs):
    return pl.pallas_call(
        columns_kernel,
        out_shape=[jax.ShapeDtypeStruct((QUADS * 32, NEL * V), BF16), jax.ShapeDtypeStruct((NBLK, V), BF16)],
        in_specs=[pl.BlockSpec(memory_space=pltpu.SMEM)] + vmem(2), out_specs=vmem(2),
        scratch_shapes=[pltpu.VMEM((NBLK, V), F32)],
        compiler_params=params(8), cost_estimate=cost(800_000_000), name="spread_first",
    )(parents, excitations, coeffs)


def spread_second(excitations, coeffs):
    return pl.pallas_call(
        functools.partial(spread_kernel, 1),
        out_shape=jax.ShapeDtypeStruct((QUADS * 32, NEL * V), BF16),
        in_specs=vmem(2), out_specs=vmem(1)[0],
        compiler_params=params(8), cost_estimate=cost(800_000_000), name="spread_second",
    )(excitations, coeffs)


def partial_values(parents, me, tables, halves, columns, excitations, coeffs):
    return pl.pallas_call(
        value_kernel,
        out_shape=[jax.ShapeDtypeStruct((8, GROUP), F32), jax.ShapeDtypeStruct((GROUP, NEL * V), BF16),
                   jax.ShapeDtypeStruct((2 * GROUP, KD), BF16), jax.ShapeDtypeStruct((NBLK * 8, GROUP), F32)],
        in_specs=[pl.BlockSpec(memory_space=pltpu.SMEM)] * 2 + vmem(NDET + 5), out_specs=vmem(4),
        scratch_shapes=[pltpu.VMEM((NBLK * JPAD, GROUP), F32), pltpu.VMEM((NBLK * STATES, GROUP), F32),
                        pltpu.VMEM((STATES, GROUP, BLOCK), F32)],
        compiler_params=params(22), name="partial_values",
    )(parents, me, *tables, *halves, columns, excitations, coeffs)


def gradient(me, parts, local_energy, excitations, tab, pair_products, tia):
    return pl.pallas_call(
        grad_kernel,
        out_shape=[jax.ShapeDtypeStruct((STATES, OWN), F32), jax.ShapeDtypeStruct((NWALK, 16, 2 * BLOCK), BF16)],
        in_specs=[pl.BlockSpec(memory_space=pltpu.SMEM)] + vmem(9), out_specs=vmem(2),
        scratch_shapes=[pltpu.VMEM((NBLK, JP * 16, 2 * V), BF16), pltpu.VMEM((4, 8, GROUP), F32)],
        compiler_params=params(20), name="gradient",
    )(me, *parts, local_energy, excitations, tab, pair_products, tia)


def finish(messages):
    return pl.pallas_call(
        final_kernel,
        out_shape=[jax.ShapeDtypeStruct((STATES, 1, 256), F32), jax.ShapeDtypeStruct((1, STATES), F32)],
        in_specs=vmem(1), out_specs=vmem(2),
        compiler_params=params(8), name="finish",
    )(messages)


def across(x, step):
    return lax.ppermute(x, "det", [(i, (i + 2 * step(i % 2)) % NDET) for i in range(NDET)])


def other_core(x):
    return lax.ppermute(x, "det", [(i, i ^ 1) for i in range(NDET)])


def shards(positions, inverse, centers, exponent, orbital_weights, excitations, state_coeffs, local_energy):
    me = jnp.stack([lax.axis_index("walk"), lax.axis_index("det")])
    parents = excitations[0:2, ::BLOCK]
    table = make_table(positions, inverse, centers, exponent, orbital_weights)
    ahead = across(table, lambda c: 1 - 2 * c)
    behind = across(table, lambda c: 2 * c - 1)
    half0, columns = spread_first(parents, excitations, state_coeffs)
    ahead, columns = lax.optimization_barrier((ahead, columns))
    beyond = across(ahead, lambda c: 1 - 2 * c)
    half1 = spread_second(excitations, state_coeffs)
    tables = [table, ahead, behind, beyond]
    tables = tables + [other_core(t) for t in tables]
    part, tab, products, tia = partial_values(parents, me, tables, (half0, half1), columns, excitations, state_coeffs)
    chip = part + other_core(part)
    parts = [chip] + [across(chip, lambda c, d=d: d) for d in (1, 2, 3)]
    own, messages = gradient(me, parts, local_energy, excitations, tab, products, tia)
    grad, energy = finish(lax.all_to_all(messages, "walk", 0, 0, tiled=True))
    return grad, own, energy.reshape(STATES)


def solution(mesh):
    in_specs = (
        P(None, ("walk", "det"), None),
        P(("walk", "det"), None, None),
        P(),
        P(),
        P(),
        P(None, "det"),
        P(None, "det"),
        P(None, "walk"),
    )
    out_specs = (P(None, "det", "walk"), P(None, ("walk", "det")), P())
    return jax.shard_map(shards, mesh=mesh, in_specs=in_specs, out_specs=out_specs, check_vma=False)
```

```python
import functools

import jax
import jax.numpy as jnp
from jax import lax
from jax.experimental import pallas as pl
from jax.experimental.pallas import tpu as pltpu
from jax.sharding import PartitionSpec as P

NEL = 50
ROWS = 56
V = 128
NBAS = 512
STATES = 4
BLOCK = 128
OWN = 16
GROUP = 128
KD = 8192
NBLK = KD // BLOCK
PAIRS = NBLK // 2
JP = NEL // 2
NDET = 8
NWALK = 32
JPAD = 64
MIB = 1024 * 1024
UNROLL = 8
QUADS = PAIRS // 4

F32, BF16 = jnp.float32, jnp.bfloat16
NN = (((1,), (0,)), ((), ()))
NT = (((1,), (1,)), ((), ()))
TN = (((0,), (0,)), ((), ()))


def dot(a, b, dims=NN):
    return lax.dot_general(a, b, dims, preferred_element_type=F32)


def split(x):
    hi = x.astype(BF16)
    return hi, (x - hi.astype(F32)).astype(BF16)


def vmem(n):
    return [pl.BlockSpec(memory_space=pltpu.VMEM)] * n


def table_kernel(pos_hbm, inv_hbm, cen_hbm, exp_hbm, orb_hbm, out_ref, pos_ref, inv_ref, cen_ref, exp_ref, orb_ref,
                 pos_s, basis_s, virt_s, inv_s, tab_s, sems):
    copies = [pltpu.make_async_copy(src, dst, sems.at[n]) for n, (src, dst) in enumerate(
        ((pos_hbm, pos_ref), (cen_hbm, cen_ref), (exp_hbm, exp_ref), (orb_hbm, orb_ref), (inv_hbm, inv_ref)))]
    for copy in copies:
        copy.start()
    pos_s[...] = jnp.zeros_like(pos_s)
    virt_s[...] = jnp.zeros_like(virt_s)
    inv_s[...] = jnp.zeros_like(inv_s)
    for copy in copies[:3]:
        copy.wait()
    for c in range(3):
        pos_s[c * OWN:(c + 1) * OWN, 0:NEL] = pos_ref[c]
    cols = pos_s[...].T
    neg = -exp_ref[...]
    for w in range(OWN):
        dist = jnp.zeros((ROWS, NBAS), F32)
        for c in range(3):
            off = cols[0:ROWS, c * OWN + w:c * OWN + w + 1] - cen_ref[c:c + 1, :]
            dist = dist + off * off
        basis_s[w * ROWS:(w + 1) * ROWS, :] = jnp.exp(neg * dist)
    b_hi, b_lo = split(basis_s[...])
    copies[3].wait()
    o_hi, o_lo = split(orb_ref[...])
    virt = dot(b_hi, o_hi) + (dot(b_hi, o_lo) + dot(b_lo, o_hi))
    for w in range(OWN):
        virt_s[w, 0:ROWS, :] = virt[w * ROWS:(w + 1) * ROWS]
    copies[4].wait()
    for w in range(OWN):
        inv_s[w, 0:NEL, 0:NEL] = inv_ref[:, w, :]
    for w in range(OWN):
        i_hi, i_lo = split(inv_s[w])
        v_hi, v_lo = split(virt_s[w])
        table = dot(i_hi, v_hi) + (dot(i_hi, v_lo) + dot(i_lo, v_hi))
        tab_s[pl.ds(w, ROWS, stride=OWN), :] = table[0:ROWS]
    for i in range(NEL):
        out_ref[:, i * V:(i + 1) * V] = tab_s[i * OWN:(i + 1) * OWN, :].astype(BF16)


def spread_kernel(side, exc_ref, coef_ref, spread_ref, oa_ref, oa_s):
    lane = lax.broadcasted_iota(jnp.int32, (1, V), 1)
    for n in range(NBLK // 2):
        blk = side * (NBLK // 2) + n
        parent = exc_ref[1:2, blk * BLOCK:(blk + 1) * BLOCK]
        oa_s[n:n + 1, :] = jnp.where(lane == parent, 1.0, 0.0).astype(F32)
    oa_ref[...] = oa_s[...].astype(BF16)
    sub_b = lax.broadcasted_iota(jnp.int32, (V, 2 * BLOCK), 0)
    half = lax.broadcasted_iota(jnp.int32, (8, 2 * BLOCK), 1) // BLOCK
    upper = lax.broadcasted_iota(jnp.int32, (8, 2 * BLOCK), 0) // STATES

    def quad(q, _):
        parts = []
        for h in range(2):
            where = pl.ds(pl.multiple_of((side * QUADS * 2 + 2 * q + h) * 2 * BLOCK, 2 * BLOCK), 2 * BLOCK)
            j_row, b_row = exc_ref[2:3, where], exc_ref[3:4, where]
            c4 = coef_ref[:, where]
            c_hi, c_lo = split(jnp.concatenate([c4, c4], axis=0))
            own = half == upper
            q_hi = jnp.where(own, c_hi.astype(F32), 0.0)
            q_lo = jnp.where(own, c_lo.astype(F32), 0.0)
            pick_b = jnp.where(sub_b == b_row, 1.0, 0.0).astype(BF16)
            w_hi, w_lo = [], []
            for jp in range(JP):
                m0, m1 = j_row == 2 * jp, j_row == 2 * jp + 1
                w_hi.append(jnp.concatenate([jnp.where(m0, q_hi, 0.0), jnp.where(m1, q_hi, 0.0)], axis=0).astype(BF16))
                w_lo.append(jnp.concatenate([jnp.where(m0, q_lo, 0.0), jnp.where(m1, q_lo, 0.0)], axis=0).astype(BF16))
            parts.append(dot(jnp.concatenate(w_hi, axis=0), pick_b, NT) + dot(jnp.concatenate(w_lo, axis=0), pick_b, NT))
        high = pl.ds(pl.multiple_of(q * 16, 16), 16)
        low = pl.ds(pl.multiple_of(QUADS * 16 + q * 16, 16), 16)
        for j in range(NEL):
            both = jnp.concatenate([parts[0][j * 8:(j + 1) * 8], parts[1][j * 8:(j + 1) * 8]], axis=0)
            hi, lo = split(both)
            spread_ref[high, j * V:(j + 1) * V] = hi
            spread_ref[low, j * V:(j + 1) * V] = lo
        return _

    lax.fori_loop(0, QUADS, quad, 0)


def value_kernel(me_ref, t0, t1, t2, t3, t4, t5, t6, t7, half0, half1, oa0, oa1, exc_ref, coef_ref,
                 part_ref, tab_ref, p_ref, tia_ref, v_s, x_s, acc_s, exc_smem, sem):
    indices = pltpu.make_async_copy(exc_ref, exc_smem, sem)
    indices.start()
    x, c = lax.shift_right_logical(me_ref[1], 1), jnp.bitwise_and(me_ref[1], 1)
    ahead = 1 - 2 * c
    sources = ((x, c), (x - ahead, c), (x + ahead, c), (x + 2, c),
               (x, 1 - c), (x + ahead, 1 - c), (x - ahead, 1 - c), (x + 2, 1 - c))
    for t_ref, (xx, cc) in zip((t0, t1, t2, t3, t4, t5, t6, t7), sources):
        source = 2 * jnp.bitwise_and(xx + 4, 3) + cc
        tab_ref[pl.ds(pl.multiple_of(source * OWN, OWN), OWN), :] = t_ref[...]
    for j in range(NEL, JPAD):
        v_s[pl.ds(j, NBLK, stride=JPAD), :] = jnp.zeros((NBLK, GROUP), F32)
    rows = QUADS * 16
    for side, half in enumerate((half0, half1)):
        x = dot(half[...], tab_ref[...], NT)
        x_s[side * rows:(side + 1) * rows, :] = x[0:rows] + x[rows:]
    pick_a = jnp.concatenate([oa0[...], oa1[...]], axis=0)
    for j in range(NEL):
        v_s[pl.ds(j, NBLK, stride=JPAD), :] = dot(pick_a, tab_ref[:, j * V:(j + 1) * V], NT)

    indices.wait()

    def own_entry(blk, _):
        row = v_s[pl.ds(blk * JPAD + exc_smem[0, blk * BLOCK], 1), :]
        tia_ref[pl.ds(pl.multiple_of(blk * 8, 8), 8), :] = jnp.broadcast_to(row, (8, GROUP))
        return _

    lax.fori_loop(0, NBLK, own_entry, 0, unroll=8)
    acc_s[...] = jnp.zeros_like(acc_s)
    low = lax.broadcasted_iota(jnp.int32, (8, GROUP), 0) < STATES
    sub_b = lax.broadcasted_iota(jnp.int32, (V, BLOCK), 0)
    sub_j = lax.broadcasted_iota(jnp.int32, (JPAD, BLOCK), 0)

    def pair(p, first):
        products = []
        for h in range(2):
            blk = 2 * p + h
            dets = pl.ds(pl.multiple_of(blk * BLOCK, BLOCK), BLOCK)
            pick_j = jnp.where(sub_j == exc_ref[2:3, dets], 1.0, 0.0).astype(BF16)
            pick_b = jnp.where(sub_b == exc_ref[3:4, dets], 1.0, 0.0).astype(BF16)
            t_i = tab_ref[:, pl.ds(pl.multiple_of(exc_smem[0, blk * BLOCK] * V, V), V)]
            along = dot(t_i, pick_b)
            column = v_s[pl.ds(pl.multiple_of(blk * JPAD, JPAD), JPAD), :].astype(BF16)
            down = dot(column, pick_j, TN)
            product = along * down
            hi, lo = split(product)
            p_ref[0:GROUP, dets] = hi
            p_ref[GROUP:2 * GROUP, dets] = lo
            products.append((product, dets))
        for s in range(STATES):
            acc_s[s] += products[0][0] * coef_ref[s:s + 1, products[0][1]] + products[1][0] * coef_ref[s:s + 1, products[1][1]]
        tia = jnp.where(low, tia_ref[pl.ds(pl.multiple_of(p * 16, 16), 8), :],
                        tia_ref[pl.ds(pl.multiple_of(p * 16 + 8, 8), 8), :])
        return first + x_s[pl.ds(pl.multiple_of(p * 8, 8), 8), :] * tia

    first = lax.fori_loop(0, PAIRS, pair, jnp.zeros((8, GROUP), F32), unroll=UNROLL)
    first = first + jnp.concatenate([first[STATES:], first[:STATES]], axis=0)
    second = jnp.concatenate([jnp.sum(acc_s[s].T, axis=0, keepdims=True) for s in range(STATES)] * 2, axis=0)
    part_ref[...] = first - second


def grad_kernel(me_ref, p0, p1, p2, p3, energy_ref, exc_ref, tab_ref, p_ref, tia_ref, own_ref, out_ref, g_s, order_s):
    me = me_ref[1]
    for d, part in enumerate((p0, p1, p2, p3)):
        order_s[jnp.bitwise_and(lax.shift_right_logical(me, 1) - d + 4, 3)] = part[...]
    val = (order_s[0] + order_s[1]) + (order_s[2] + order_s[3])
    own = val[0:STATES, 0:OWN]
    for d in range(1, NDET):
        own = jnp.where(me == d, val[0:STATES, d * OWN:(d + 1) * OWN], own)
    own_ref[...] = own
    low = lax.broadcasted_iota(jnp.int32, (8, GROUP), 0) < STATES
    lane = lax.broadcasted_iota(jnp.int32, (8, GROUP), 1)
    square = val * val
    guide = 1.0 + jnp.sum(jnp.where(low, square, 0.0), axis=0, keepdims=True)
    energy = jnp.concatenate([energy_ref[...], energy_ref[...]], axis=0)
    middle = jnp.sum(energy, axis=1, keepdims=True) * (1.0 / GROUP)
    scaled = val / guide
    weight = square / guide
    sums = jnp.sum(jnp.where(low, weight, weight * energy), axis=1, keepdims=True)
    meta = jnp.zeros((8, GROUP), F32)
    for at, value in ((0, sums), (3, middle)):
        for n in range(3):
            piece = value.astype(BF16).astype(F32)
            meta = jnp.where(lane == at + n, piece, meta)
            value = value - piece
    meta = jnp.concatenate([meta, meta], axis=0).astype(BF16)
    factor = jnp.where(low, scaled * (energy - middle), scaled)
    f_hi, f_lo = split(factor)
    f16 = jnp.concatenate([f_hi.astype(F32), f_lo.astype(F32)], axis=0).astype(BF16)
    f16 = jnp.concatenate([f16, f16], axis=1)
    lhs = tia_ref[...].reshape(NBLK, 8, GROUP) * factor[None]
    l_hi, l_lo = split(lhs.reshape(NBLK * 8, GROUP))
    lhs = jnp.concatenate([l_hi, l_lo], axis=1)

    for jp in range(JP):
        t = tab_ref[:, jp * 2 * V:(jp + 1) * 2 * V]
        g = dot(lhs, jnp.concatenate([t, t], axis=0)).reshape(NBLK, 8, 2 * V)
        hi, lo = split(jnp.concatenate([g[:, :, 0:V], g[:, :, V:2 * V]], axis=1))
        g_s[:, jp * 16:(jp + 1) * 16, 0:V] = hi
        g_s[:, jp * 16:(jp + 1) * 16, V:2 * V] = lo
    sub_b = lax.broadcasted_iota(jnp.int32, (V, BLOCK), 0)

    def slot(p, _):
        both = pl.ds(pl.multiple_of(p * 2 * BLOCK, 2 * BLOCK), 2 * BLOCK)
        second = dot(f16, p_ref[:, both])
        second = second[0:8] + second[8:16]
        terms = []
        for h in range(2):
            dets = pl.ds(pl.multiple_of(p * 2 * BLOCK + h * BLOCK, BLOCK), BLOCK)
            j_row, b_row = exc_ref[2:3, dets], exc_ref[3:4, dets]
            pick_b = jnp.where(sub_b == b_row, 1.0, 0.0).astype(BF16)
            y = dot(g_s[2 * p + h], jnp.concatenate([pick_b, pick_b], axis=0))
            first = jnp.zeros((8, BLOCK), F32)
            for j in range(NEL):
                first = jnp.where(j_row == j, y[j * 8:(j + 1) * 8], first)
            terms.append(first - second[:, h * BLOCK:(h + 1) * BLOCK])
        out_ref[p, :, 0:BLOCK] = jnp.concatenate(terms, axis=0).astype(BF16)
        out_ref[p, :, BLOCK:2 * BLOCK] = meta
        return _

    lax.fori_loop(0, NWALK, slot, 0, unroll=UNROLL)


def final_kernel(in_ref, grad_ref, energy_ref):
    lane = lax.broadcasted_iota(jnp.int32, (8, BLOCK), 1)
    metas = [in_ref[g].astype(F32)[0:8, BLOCK:2 * BLOCK] for g in range(NWALK)]
    meta = metas[0]
    for g in range(1, NWALK):
        meta = meta + metas[g]
    sums = jnp.sum(jnp.where(lane < 3, meta, 0.0), axis=1, keepdims=True)
    total, weighted = sums[0:STATES], sums[STATES:8]
    energy = weighted / total
    grads = [jnp.zeros((STATES, BLOCK), F32)] * 2
    for g in range(NWALK):
        terms = in_ref[g].astype(F32)
        middle = jnp.sum(jnp.where((lane >= 3) & (lane < 6), metas[g], 0.0), axis=1, keepdims=True)
        shift = middle[0:STATES] - energy
        for h in range(2):
            grads[h] = grads[h] + (terms[h * 8:h * 8 + STATES, 0:BLOCK]
                                   + shift * terms[h * 8 + STATES:h * 8 + 8, 0:BLOCK])
    scale = 2.0 / total
    grad_ref[:, 0, 0:BLOCK] = grads[0] * scale
    grad_ref[:, 0, BLOCK:2 * BLOCK] = grads[1] * scale
    place = lax.broadcasted_iota(jnp.int32, (STATES, STATES), 0) == lax.broadcasted_iota(jnp.int32, (STATES, STATES), 1)
    energy_ref[...] = jnp.sum(jnp.where(place, energy, 0.0), axis=0, keepdims=True)


def params(mib):
    return pltpu.CompilerParams(vmem_limit_bytes=mib * MIB)


def make_table(positions, inverse, centers, exponent, orbital_weights):
    return pl.pallas_call(
        table_kernel,
        out_shape=jax.ShapeDtypeStruct((OWN, NEL * V), BF16),
        in_specs=[pl.BlockSpec(memory_space=pltpu.HBM)] * 5, out_specs=vmem(1)[0],
        scratch_shapes=[pltpu.VMEM((3, OWN, NEL), F32), pltpu.VMEM((NEL, OWN, NEL), F32), pltpu.VMEM((3, NBAS), F32),
                        pltpu.VMEM((1, NBAS), F32), pltpu.VMEM((NBAS, V), F32), pltpu.VMEM((128, 128), F32), pltpu.VMEM((OWN * ROWS, NBAS), F32),
                        pltpu.VMEM((OWN, 128, V), F32), pltpu.VMEM((OWN, JPAD, 128), F32),
                        pltpu.VMEM((ROWS * OWN, V), F32), pltpu.SemaphoreType.DMA((5,))],
        compiler_params=params(60), name="tables",
    )(positions, inverse.transpose(1, 0, 2), centers, exponent.reshape(1, NBAS), orbital_weights)


def cost(flops):
    return pl.CostEstimate(flops=flops, bytes_accessed=8 * MIB, transcendentals=0)


def spread(side, excitations, coeffs):
    return pl.pallas_call(
        functools.partial(spread_kernel, side),
        out_shape=[jax.ShapeDtypeStruct((QUADS * 32, NEL * V), BF16), jax.ShapeDtypeStruct((NBLK // 2, V), BF16)],
        in_specs=vmem(2), out_specs=vmem(2),
        scratch_shapes=[pltpu.VMEM((NBLK // 2, V), F32)],
        compiler_params=params(8), cost_estimate=cost(800_000_000), name="spread",
    )(excitations, coeffs)


def partial_values(me, tables, halves, columns, excitations, coeffs):
    return pl.pallas_call(
        value_kernel,
        out_shape=[jax.ShapeDtypeStruct((8, GROUP), F32), jax.ShapeDtypeStruct((GROUP, NEL * V), BF16),
                   jax.ShapeDtypeStruct((2 * GROUP, KD), BF16), jax.ShapeDtypeStruct((NBLK * 8, GROUP), F32)],
        in_specs=[pl.BlockSpec(memory_space=pltpu.SMEM)] + vmem(NDET + 6), out_specs=vmem(4),
        scratch_shapes=[pltpu.VMEM((NBLK * JPAD, GROUP), F32), pltpu.VMEM((NBLK * STATES, GROUP), F32),
                        pltpu.VMEM((STATES, GROUP, BLOCK), F32),
                        pltpu.SMEM((4, KD), jnp.int32), pltpu.SemaphoreType.DMA],
        compiler_params=params(22), name="partial_values",
    )(me, *tables, *halves, *columns, excitations, coeffs)


def gradient(me, parts, local_energy, excitations, tab, pair_products, tia):
    return pl.pallas_call(
        grad_kernel,
        out_shape=[jax.ShapeDtypeStruct((STATES, OWN), F32), jax.ShapeDtypeStruct((NWALK, 16, 2 * BLOCK), BF16)],
        in_specs=[pl.BlockSpec(memory_space=pltpu.SMEM)] + vmem(9), out_specs=vmem(2),
        scratch_shapes=[pltpu.VMEM((NBLK, JP * 16, 2 * V), BF16), pltpu.VMEM((4, 8, GROUP), F32)],
        compiler_params=params(20), name="gradient",
    )(me, *parts, local_energy, excitations, tab, pair_products, tia)


def finish(messages):
    return pl.pallas_call(
        final_kernel,
        out_shape=[jax.ShapeDtypeStruct((STATES, 1, 256), F32), jax.ShapeDtypeStruct((1, STATES), F32)],
        in_specs=vmem(1), out_specs=vmem(2),
        compiler_params=params(8), name="finish",
    )(messages)


def across(x, step):
    return lax.ppermute(x, "det", [(i, (i + 2 * step(i % 2)) % NDET) for i in range(NDET)])


def other_core(x):
    return lax.ppermute(x, "det", [(i, i ^ 1) for i in range(NDET)])


def shards(positions, inverse, centers, exponent, orbital_weights, excitations, state_coeffs, local_energy):
    me = jnp.stack([lax.axis_index("walk"), lax.axis_index("det")])
    table = make_table(positions, inverse, centers, exponent, orbital_weights)
    ahead = across(table, lambda c: 1 - 2 * c)
    behind = across(table, lambda c: 2 * c - 1)
    half0, columns0 = spread(0, excitations, state_coeffs)
    ahead, columns0 = lax.optimization_barrier((ahead, columns0))
    beyond = across(ahead, lambda c: 1 - 2 * c)
    half1, columns1 = spread(1, excitations, state_coeffs)
    near = [other_core(t) for t in (table, ahead, behind)]
    tables = [table, ahead, behind, beyond] + near + [other_core(beyond)]
    part, tab, products, tia = partial_values(me, tables, (half0, half1), (columns0, columns1), excitations, state_coeffs)
    chip = part + other_core(part)
    parts = [chip] + [across(chip, lambda c, d=d: d) for d in (1, 2, 3)]
    own, messages = gradient(me, parts, local_energy, excitations, tab, products, tia)
    grad, energy = finish(lax.all_to_all(messages, "walk", 0, 0, tiled=True))
    return grad, own, energy.reshape(STATES)


def solution(mesh):
    in_specs = (
        P(None, ("walk", "det"), None),
        P(("walk", "det"), None, None),
        P(),
        P(),
        P(),
        P(None, "det"),
        P(None, "det"),
        P(None, "walk"),
    )
    out_specs = (P(None, "det", "walk"), P(None, ("walk", "det")), P())
    return jax.shard_map(shards, mesh=mesh, in_specs=in_specs, out_specs=out_specs, check_vma=False)
```

```python
import functools

import jax
import jax.numpy as jnp
from jax import lax
from jax.experimental import pallas as pl
from jax.experimental.pallas import tpu as pltpu
from jax.sharding import PartitionSpec as P

NEL = 50
ROWS = 56
V = 128
NBAS = 512
STATES = 4
BLOCK = 128
OWN = 16
GROUP = 128
KD = 8192
NBLK = KD // BLOCK
PAIRS = NBLK // 2
JP = NEL // 2
NDET = 8
NWALK = 32
JPAD = 64
MIB = 1024 * 1024
UNROLL = 8
QUADS = PAIRS // 4

F32, BF16 = jnp.float32, jnp.bfloat16
NN = (((1,), (0,)), ((), ()))
NT = (((1,), (1,)), ((), ()))
TN = (((0,), (0,)), ((), ()))


def dot(a, b, dims=NN):
    return lax.dot_general(a, b, dims, preferred_element_type=F32)


def split(x):
    hi = x.astype(BF16)
    return hi, (x - hi.astype(F32)).astype(BF16)


def vmem(n):
    return [pl.BlockSpec(memory_space=pltpu.VMEM)] * n


def table_kernel(pos_hbm, inv_hbm, cen_hbm, exp_hbm, orb_hbm, out_ref, pos_ref, inv_ref, cen_ref, exp_ref, orb_ref,
                 pos_s, basis_s, virt_s, inv_s, tab_s, sems):
    copies = [pltpu.make_async_copy(src, dst, sems.at[n]) for n, (src, dst) in enumerate(
        ((pos_hbm, pos_ref), (cen_hbm, cen_ref), (exp_hbm, exp_ref), (orb_hbm, orb_ref), (inv_hbm, inv_ref)))]
    for copy in copies:
        copy.start()
    pos_s[...] = jnp.zeros_like(pos_s)
    virt_s[...] = jnp.zeros_like(virt_s)
    inv_s[...] = jnp.zeros_like(inv_s)
    for copy in copies[:3]:
        copy.wait()
    for c in range(3):
        pos_s[c * OWN:(c + 1) * OWN, 0:NEL] = pos_ref[c]
    cols = pos_s[...].T
    neg = -exp_ref[...]
    for w in range(OWN):
        dist = jnp.zeros((ROWS, NBAS), F32)
        for c in range(3):
            off = cols[0:ROWS, c * OWN + w:c * OWN + w + 1] - cen_ref[c:c + 1, :]
            dist = dist + off * off
        basis_s[w * ROWS:(w + 1) * ROWS, :] = jnp.exp(neg * dist)
    b_hi, b_lo = split(basis_s[...])
    copies[3].wait()
    o_hi, o_lo = split(orb_ref[...])
    virt = dot(b_hi, o_hi) + (dot(b_hi, o_lo) + dot(b_lo, o_hi))
    for w in range(OWN):
        virt_s[w, 0:ROWS, :] = virt[w * ROWS:(w + 1) * ROWS]
    copies[4].wait()
    for w in range(OWN):
        inv_s[w, 0:NEL, 0:NEL] = inv_ref[:, w, :]
    for w in range(OWN):
        i_hi, i_lo = split(inv_s[w])
        v_hi, v_lo = split(virt_s[w])
        table = dot(i_hi, v_hi) + (dot(i_hi, v_lo) + dot(i_lo, v_hi))
        tab_s[pl.ds(w, ROWS, stride=OWN), :] = table[0:ROWS]
    for i in range(NEL):
        out_ref[:, i * V:(i + 1) * V] = tab_s[i * OWN:(i + 1) * OWN, :].astype(BF16)


def first_kernel(exc_ref, coef_ref, spread_ref, oa_ref, exc_out, coef_out, oa_s):
    exc_out[...] = exc_ref[...]
    coef_out[...] = coef_ref[...]
    spread_kernel(0, exc_ref, coef_ref, spread_ref, oa_ref, oa_s)


def spread_kernel(side, exc_ref, coef_ref, spread_ref, oa_ref, oa_s):
    lane = lax.broadcasted_iota(jnp.int32, (1, V), 1)
    for n in range(NBLK // 2):
        blk = side * (NBLK // 2) + n
        parent = exc_ref[1:2, blk * BLOCK:(blk + 1) * BLOCK]
        oa_s[n:n + 1, :] = jnp.where(lane == parent, 1.0, 0.0).astype(F32)
    oa_ref[...] = oa_s[...].astype(BF16)
    sub_b = lax.broadcasted_iota(jnp.int32, (V, 2 * BLOCK), 0)
    half = lax.broadcasted_iota(jnp.int32, (8, 2 * BLOCK), 1) // BLOCK
    upper = lax.broadcasted_iota(jnp.int32, (8, 2 * BLOCK), 0) // STATES

    def quad(q, _):
        parts = []
        for h in range(2):
            where = pl.ds(pl.multiple_of((side * QUADS * 2 + 2 * q + h) * 2 * BLOCK, 2 * BLOCK), 2 * BLOCK)
            j_row, b_row = exc_ref[2:3, where], exc_ref[3:4, where]
            c4 = coef_ref[:, where]
            c_hi, c_lo = split(jnp.concatenate([c4, c4], axis=0))
            own = half == upper
            q_hi = jnp.where(own, c_hi.astype(F32), 0.0)
            q_lo = jnp.where(own, c_lo.astype(F32), 0.0)
            pick_b = jnp.where(sub_b == b_row, 1.0, 0.0).astype(BF16)
            w_hi, w_lo = [], []
            for jp in range(JP):
                m0, m1 = j_row == 2 * jp, j_row == 2 * jp + 1
                w_hi.append(jnp.concatenate([jnp.where(m0, q_hi, 0.0), jnp.where(m1, q_hi, 0.0)], axis=0).astype(BF16))
                w_lo.append(jnp.concatenate([jnp.where(m0, q_lo, 0.0), jnp.where(m1, q_lo, 0.0)], axis=0).astype(BF16))
            parts.append(dot(jnp.concatenate(w_hi, axis=0), pick_b, NT) + dot(jnp.concatenate(w_lo, axis=0), pick_b, NT))
        high = pl.ds(pl.multiple_of(q * 16, 16), 16)
        low = pl.ds(pl.multiple_of(QUADS * 16 + q * 16, 16), 16)
        for j in range(NEL):
            both = jnp.concatenate([parts[0][j * 8:(j + 1) * 8], parts[1][j * 8:(j + 1) * 8]], axis=0)
            hi, lo = split(both)
            spread_ref[high, j * V:(j + 1) * V] = hi
            spread_ref[low, j * V:(j + 1) * V] = lo
        return _

    lax.fori_loop(0, QUADS, quad, 0)


def value_kernel(me_ref, t0, t1, t2, t3, t4, t5, t6, t7, half0, half1, oa0, oa1, exc_ref, coef_ref,
                 part_ref, tab_ref, p_ref, tia_ref, v_s, x_s, acc_s, exc_smem, sem):
    indices = pltpu.make_async_copy(exc_ref.at[0:1, :], exc_smem, sem)
    indices.start()
    x, c = lax.shift_right_logical(me_ref[1], 1), jnp.bitwise_and(me_ref[1], 1)
    ahead = 1 - 2 * c
    sources = ((x, c), (x - ahead, c), (x + ahead, c), (x + 2, c),
               (x, 1 - c), (x + ahead, 1 - c), (x - ahead, 1 - c), (x + 2, 1 - c))
    for t_ref, (xx, cc) in zip((t0, t1, t2, t3, t4, t5, t6, t7), sources):
        source = 2 * jnp.bitwise_and(xx + 4, 3) + cc
        tab_ref[pl.ds(pl.multiple_of(source * OWN, OWN), OWN), :] = t_ref[...]
    for j in range(NEL, JPAD):
        v_s[pl.ds(j, NBLK, stride=JPAD), :] = jnp.zeros((NBLK, GROUP), F32)
    rows = QUADS * 16
    for side, half in enumerate((half0, half1)):
        x = dot(half[...], tab_ref[...], NT)
        x_s[side * rows:(side + 1) * rows, :] = x[0:rows] + x[rows:]
    pick_a = jnp.concatenate([oa0[...], oa1[...]], axis=0)
    for j in range(NEL):
        v_s[pl.ds(j, NBLK, stride=JPAD), :] = dot(pick_a, tab_ref[:, j * V:(j + 1) * V], NT)

    indices.wait()

    def own_entry(blk, _):
        row = v_s[pl.ds(blk * JPAD + exc_smem[0, blk * BLOCK], 1), :]
        tia_ref[pl.ds(pl.multiple_of(blk * 8, 8), 8), :] = jnp.broadcast_to(row, (8, GROUP))
        return _

    lax.fori_loop(0, NBLK, own_entry, 0, unroll=8)
    acc_s[...] = jnp.zeros_like(acc_s)
    low = lax.broadcasted_iota(jnp.int32, (8, GROUP), 0) < STATES
    sub_b = lax.broadcasted_iota(jnp.int32, (V, BLOCK), 0)
    sub_j = lax.broadcasted_iota(jnp.int32, (JPAD, BLOCK), 0)

    def pair(p, first):
        products = []
        for h in range(2):
            blk = 2 * p + h
            dets = pl.ds(pl.multiple_of(blk * BLOCK, BLOCK), BLOCK)
            pick_j = jnp.where(sub_j == exc_ref[2:3, dets], 1.0, 0.0).astype(BF16)
            pick_b = jnp.where(sub_b == exc_ref[3:4, dets], 1.0, 0.0).astype(BF16)
            t_i = tab_ref[:, pl.ds(pl.multiple_of(exc_smem[0, blk * BLOCK] * V, V), V)]
            along = dot(t_i, pick_b)
            column = v_s[pl.ds(pl.multiple_of(blk * JPAD, JPAD), JPAD), :].astype(BF16)
            down = dot(column, pick_j, TN)
            product = along * down
            hi, lo = split(product)
            p_ref[0:GROUP, dets] = hi
            p_ref[GROUP:2 * GROUP, dets] = lo
            products.append((product, dets))
        for s in range(STATES):
            acc_s[s] += products[0][0] * coef_ref[s:s + 1, products[0][1]] + products[1][0] * coef_ref[s:s + 1, products[1][1]]
        tia = jnp.where(low, tia_ref[pl.ds(pl.multiple_of(p * 16, 16), 8), :],
                        tia_ref[pl.ds(pl.multiple_of(p * 16 + 8, 8), 8), :])
        return first + x_s[pl.ds(pl.multiple_of(p * 8, 8), 8), :] * tia

    first = lax.fori_loop(0, PAIRS, pair, jnp.zeros((8, GROUP), F32), unroll=UNROLL)
    first = first + jnp.concatenate([first[STATES:], first[:STATES]], axis=0)
    second = jnp.concatenate([jnp.sum(acc_s[s].T, axis=0, keepdims=True) for s in range(STATES)] * 2, axis=0)
    part_ref[...] = first - second


def grad_kernel(me_ref, p0, p1, p2, p3, energy_ref, exc_ref, tab_ref, p_ref, tia_ref, own_ref, out_ref, g_s, order_s):
    me = me_ref[1]
    for d, part in enumerate((p0, p1, p2, p3)):
        order_s[jnp.bitwise_and(lax.shift_right_logical(me, 1) - d + 4, 3)] = part[...]
    val = (order_s[0] + order_s[1]) + (order_s[2] + order_s[3])
    own = val[0:STATES, 0:OWN]
    for d in range(1, NDET):
        own = jnp.where(me == d, val[0:STATES, d * OWN:(d + 1) * OWN], own)
    own_ref[...] = own
    low = lax.broadcasted_iota(jnp.int32, (8, GROUP), 0) < STATES
    lane = lax.broadcasted_iota(jnp.int32, (8, GROUP), 1)
    square = val * val
    guide = 1.0 + jnp.sum(jnp.where(low, square, 0.0), axis=0, keepdims=True)
    energy = jnp.concatenate([energy_ref[...], energy_ref[...]], axis=0)
    middle = jnp.sum(energy, axis=1, keepdims=True) * (1.0 / GROUP)
    scaled = val / guide
    weight = square / guide
    sums = jnp.sum(jnp.where(low, weight, weight * energy), axis=1, keepdims=True)
    meta = jnp.zeros((8, GROUP), F32)
    for at, value in ((0, sums), (3, middle)):
        for n in range(3):
            piece = value.astype(BF16).astype(F32)
            meta = jnp.where(lane == at + n, piece, meta)
            value = value - piece
    meta = jnp.concatenate([meta, meta], axis=0).astype(BF16)
    factor = jnp.where(low, scaled * (energy - middle), scaled)
    f_hi, f_lo = split(factor)
    f16 = jnp.concatenate([f_hi.astype(F32), f_lo.astype(F32)], axis=0).astype(BF16)
    f16 = jnp.concatenate([f16, f16], axis=1)
    lhs = tia_ref[...].reshape(NBLK, 8, GROUP) * factor[None]
    l_hi, l_lo = split(lhs.reshape(NBLK * 8, GROUP))
    lhs = jnp.concatenate([l_hi, l_lo], axis=1)

    for jp in range(JP):
        t = tab_ref[:, jp * 2 * V:(jp + 1) * 2 * V]
        g = dot(lhs, jnp.concatenate([t, t], axis=0)).reshape(NBLK, 8, 2 * V)
        hi, lo = split(jnp.concatenate([g[:, :, 0:V], g[:, :, V:2 * V]], axis=1))
        g_s[:, jp * 16:(jp + 1) * 16, 0:V] = hi
        g_s[:, jp * 16:(jp + 1) * 16, V:2 * V] = lo
    sub_b = lax.broadcasted_iota(jnp.int32, (V, BLOCK), 0)

    def slot(p, _):
        both = pl.ds(pl.multiple_of(p * 2 * BLOCK, 2 * BLOCK), 2 * BLOCK)
        second = dot(f16, p_ref[:, both])
        second = second[0:8] + second[8:16]
        terms = []
        for h in range(2):
            dets = pl.ds(pl.multiple_of(p * 2 * BLOCK + h * BLOCK, BLOCK), BLOCK)
            j_row, b_row = exc_ref[2:3, dets], exc_ref[3:4, dets]
            pick_b = jnp.where(sub_b == b_row, 1.0, 0.0).astype(BF16)
            y = dot(g_s[2 * p + h], jnp.concatenate([pick_b, pick_b], axis=0))
            first = jnp.zeros((8, BLOCK), F32)
            for j in range(NEL):
                first = jnp.where(j_row == j, y[j * 8:(j + 1) * 8], first)
            terms.append(first - second[:, h * BLOCK:(h + 1) * BLOCK])
        out_ref[p, :, 0:BLOCK] = jnp.concatenate(terms, axis=0).astype(BF16)
        out_ref[p, :, BLOCK:2 * BLOCK] = meta
        return _

    lax.fori_loop(0, NWALK, slot, 0, unroll=UNROLL)


def final_kernel(in_ref, grad_ref, energy_ref):
    lane = lax.broadcasted_iota(jnp.int32, (8, BLOCK), 1)
    metas = [in_ref[g].astype(F32)[0:8, BLOCK:2 * BLOCK] for g in range(NWALK)]
    meta = metas[0]
    for g in range(1, NWALK):
        meta = meta + metas[g]
    sums = jnp.sum(jnp.where(lane < 3, meta, 0.0), axis=1, keepdims=True)
    total, weighted = sums[0:STATES], sums[STATES:8]
    energy = weighted / total
    grads = [jnp.zeros((STATES, BLOCK), F32)] * 2
    for g in range(NWALK):
        terms = in_ref[g].astype(F32)
        middle = jnp.sum(jnp.where((lane >= 3) & (lane < 6), metas[g], 0.0), axis=1, keepdims=True)
        shift = middle[0:STATES] - energy
        for h in range(2):
            grads[h] = grads[h] + (terms[h * 8:h * 8 + STATES, 0:BLOCK]
                                   + shift * terms[h * 8 + STATES:h * 8 + 8, 0:BLOCK])
    scale = 2.0 / total
    grad_ref[:, 0, 0:BLOCK] = grads[0] * scale
    grad_ref[:, 0, BLOCK:2 * BLOCK] = grads[1] * scale
    place = lax.broadcasted_iota(jnp.int32, (STATES, STATES), 0) == lax.broadcasted_iota(jnp.int32, (STATES, STATES), 1)
    energy_ref[...] = jnp.sum(jnp.where(place, energy, 0.0), axis=0, keepdims=True)


def params(mib):
    return pltpu.CompilerParams(vmem_limit_bytes=mib * MIB)


def make_table(positions, inverse, centers, exponent, orbital_weights):
    return pl.pallas_call(
        table_kernel,
        out_shape=jax.ShapeDtypeStruct((OWN, NEL * V), BF16),
        in_specs=[pl.BlockSpec(memory_space=pltpu.HBM)] * 5, out_specs=vmem(1)[0],
        scratch_shapes=[pltpu.VMEM((3, OWN, NEL), F32), pltpu.VMEM((NEL, OWN, NEL), F32), pltpu.VMEM((3, NBAS), F32),
                        pltpu.VMEM((1, NBAS), F32), pltpu.VMEM((NBAS, V), F32), pltpu.VMEM((128, 128), F32), pltpu.VMEM((OWN * ROWS, NBAS), F32),
                        pltpu.VMEM((OWN, 128, V), F32), pltpu.VMEM((OWN, JPAD, 128), F32),
                        pltpu.VMEM((ROWS * OWN, V), F32), pltpu.SemaphoreType.DMA((5,))],
        compiler_params=params(60), name="tables",
    )(positions, inverse.transpose(1, 0, 2), centers, exponent.reshape(1, NBAS), orbital_weights)


def cost(flops):
    return pl.CostEstimate(flops=flops, bytes_accessed=8 * MIB, transcendentals=0)


def spread_first(excitations, coeffs):
    return pl.pallas_call(
        first_kernel,
        out_shape=[jax.ShapeDtypeStruct((QUADS * 32, NEL * V), BF16), jax.ShapeDtypeStruct((NBLK // 2, V), BF16),
                   jax.ShapeDtypeStruct((4, KD), jnp.int32), jax.ShapeDtypeStruct((4, KD), F32)],
        in_specs=vmem(2), out_specs=vmem(4),
        scratch_shapes=[pltpu.VMEM((NBLK // 2, V), F32)],
        compiler_params=params(8), cost_estimate=cost(50_000_000), name="spread_first",
    )(excitations, coeffs)


def spread(side, excitations, coeffs):
    return pl.pallas_call(
        functools.partial(spread_kernel, side),
        out_shape=[jax.ShapeDtypeStruct((QUADS * 32, NEL * V), BF16), jax.ShapeDtypeStruct((NBLK // 2, V), BF16)],
        in_specs=vmem(2), out_specs=vmem(2),
        scratch_shapes=[pltpu.VMEM((NBLK // 2, V), F32)],
        compiler_params=params(8), cost_estimate=cost(50_000_000), name="spread",
    )(excitations, coeffs)


def partial_values(me, tables, halves, columns, excitations, coeffs):
    return pl.pallas_call(
        value_kernel,
        out_shape=[jax.ShapeDtypeStruct((8, GROUP), F32), jax.ShapeDtypeStruct((GROUP, NEL * V), BF16),
                   jax.ShapeDtypeStruct((2 * GROUP, KD), BF16), jax.ShapeDtypeStruct((NBLK * 8, GROUP), F32)],
        in_specs=[pl.BlockSpec(memory_space=pltpu.SMEM)] + vmem(NDET + 6), out_specs=vmem(4),
        scratch_shapes=[pltpu.VMEM((NBLK * JPAD, GROUP), F32), pltpu.VMEM((NBLK * STATES, GROUP), F32),
                        pltpu.VMEM((STATES, GROUP, BLOCK), F32),
                        pltpu.SMEM((1, KD), jnp.int32), pltpu.SemaphoreType.DMA],
        compiler_params=params(22), name="partial_values",
    )(me, *tables, *halves, *columns, excitations, coeffs)


def gradient(me, parts, local_energy, excitations, tab, pair_products, tia):
    return pl.pallas_call(
        grad_kernel,
        out_shape=[jax.ShapeDtypeStruct((STATES, OWN), F32), jax.ShapeDtypeStruct((NWALK, 16, 2 * BLOCK), BF16)],
        in_specs=[pl.BlockSpec(memory_space=pltpu.SMEM)] + vmem(9), out_specs=vmem(2),
        scratch_shapes=[pltpu.VMEM((NBLK, JP * 16, 2 * V), BF16), pltpu.VMEM((4, 8, GROUP), F32)],
        compiler_params=params(20), name="gradient",
    )(me, *parts, local_energy, excitations, tab, pair_products, tia)


def finish(messages):
    return pl.pallas_call(
        final_kernel,
        out_shape=[jax.ShapeDtypeStruct((STATES, 1, 256), F32), jax.ShapeDtypeStruct((1, STATES), F32)],
        in_specs=vmem(1), out_specs=vmem(2),
        compiler_params=params(8), name="finish",
    )(messages)


def across(x, step):
    return lax.ppermute(x, "det", [(i, (i + 2 * step(i % 2)) % NDET) for i in range(NDET)])


def other_core(x):
    return lax.ppermute(x, "det", [(i, i ^ 1) for i in range(NDET)])


def shards(positions, inverse, centers, exponent, orbital_weights, excitations, state_coeffs, local_energy):
    me = jnp.stack([lax.axis_index("walk"), lax.axis_index("det")])
    table = make_table(positions, inverse, centers, exponent, orbital_weights)
    ahead = across(table, lambda c: 1 - 2 * c)
    behind = across(table, lambda c: 2 * c - 1)
    half0, columns0, excitations, state_coeffs = spread_first(excitations, state_coeffs)
    ahead, columns0 = lax.optimization_barrier((ahead, columns0))
    beyond = across(ahead, lambda c: 1 - 2 * c)
    half1, columns1 = spread(1, excitations, state_coeffs)
    near = [other_core(t) for t in (table, ahead, behind)]
    tables = [table, ahead, behind, beyond] + near + [other_core(beyond)]
    part, tab, products, tia = partial_values(me, tables, (half0, half1), (columns0, columns1), excitations, state_coeffs)
    chip = part + other_core(part)
    parts = [chip] + [across(chip, lambda c, d=d: d) for d in (1, 2, 3)]
    own, messages = gradient(me, parts, local_energy, excitations, tab, products, tia)
    grad, energy = finish(lax.all_to_all(messages, "walk", 0, 0, tiled=True))
    return grad, own, energy.reshape(STATES)


def solution(mesh):
    in_specs = (
        P(None, ("walk", "det"), None),
        P(("walk", "det"), None, None),
        P(),
        P(),
        P(),
        P(None, "det"),
        P(None, "det"),
        P(None, "walk"),
    )
    out_specs = (P(None, "det", "walk"), P(None, ("walk", "det")), P())
    return jax.shard_map(shards, mesh=mesh, in_specs=in_specs, out_specs=out_specs, check_vma=False)
```

```python
import functools

import jax
import jax.numpy as jnp
from jax import lax
from jax.experimental import pallas as pl
from jax.experimental.pallas import tpu as pltpu
from jax.sharding import PartitionSpec as P

NEL = 50
ROWS = 56
V = 128
NBAS = 512
STATES = 4
BLOCK = 128
OWN = 16
GROUP = 128
KD = 8192
NBLK = KD // BLOCK
PAIRS = NBLK // 2
JP = NEL // 2
NDET = 8
NWALK = 32
JPAD = 64
MIB = 1024 * 1024
UNROLL = 16
QUADS = PAIRS // 4

F32, BF16 = jnp.float32, jnp.bfloat16
NN = (((1,), (0,)), ((), ()))
NT = (((1,), (1,)), ((), ()))
TN = (((0,), (0,)), ((), ()))


def dot(a, b, dims=NN):
    return lax.dot_general(a, b, dims, preferred_element_type=F32)


def split(x):
    hi = x.astype(BF16)
    return hi, (x - hi.astype(F32)).astype(BF16)


def vmem(n):
    return [pl.BlockSpec(memory_space=pltpu.VMEM)] * n


def table_kernel(pos_hbm, inv_hbm, cen_hbm, exp_hbm, orb_hbm, out_ref, pos_ref, inv_ref, cen_ref, exp_ref, orb_ref,
                 pos_s, basis_s, virt_s, inv_s, tab_s, sems):
    copies = [pltpu.make_async_copy(src, dst, sems.at[n]) for n, (src, dst) in enumerate(
        ((pos_hbm, pos_ref), (cen_hbm, cen_ref), (exp_hbm, exp_ref), (orb_hbm, orb_ref), (inv_hbm, inv_ref)))]
    for copy in copies:
        copy.start()
    pos_s[...] = jnp.zeros_like(pos_s)
    virt_s[...] = jnp.zeros_like(virt_s)
    inv_s[...] = jnp.zeros_like(inv_s)
    for copy in copies[:3]:
        copy.wait()
    for c in range(3):
        pos_s[c * OWN:(c + 1) * OWN, 0:NEL] = pos_ref[c]
    cols = pos_s[...].T
    neg = -exp_ref[...]
    for w in range(OWN):
        dist = jnp.zeros((ROWS, NBAS), F32)
        for c in range(3):
            off = cols[0:ROWS, c * OWN + w:c * OWN + w + 1] - cen_ref[c:c + 1, :]
            dist = dist + off * off
        basis_s[w * ROWS:(w + 1) * ROWS, :] = jnp.exp(neg * dist)
    b_hi, b_lo = split(basis_s[...])
    copies[3].wait()
    o_hi, o_lo = split(orb_ref[...])
    virt = dot(b_hi, o_hi) + (dot(b_hi, o_lo) + dot(b_lo, o_hi))
    for w in range(OWN):
        virt_s[w, 0:ROWS, :] = virt[w * ROWS:(w + 1) * ROWS]
    copies[4].wait()
    for w in range(OWN):
        inv_s[w, 0:NEL, 0:NEL] = inv_ref[:, w, :]
    for w in range(OWN):
        i_hi, i_lo = split(inv_s[w])
        v_hi, v_lo = split(virt_s[w])
        table = dot(i_hi, v_hi) + (dot(i_hi, v_lo) + dot(i_lo, v_hi))
        tab_s[pl.ds(w, ROWS, stride=OWN), :] = table[0:ROWS]
    for i in range(NEL):
        out_ref[:, i * V:(i + 1) * V] = tab_s[i * OWN:(i + 1) * OWN, :].astype(BF16)


def first_kernel(exc_ref, coef_ref, spread_ref, oa_ref, exc_out, coef_out, oa_s):
    exc_out[...] = exc_ref[...]
    coef_out[...] = coef_ref[...]
    spread_kernel(0, exc_ref, coef_ref, spread_ref, oa_ref, oa_s)


def spread_kernel(side, exc_ref, coef_ref, spread_ref, oa_ref, oa_s):
    lane = lax.broadcasted_iota(jnp.int32, (1, V), 1)
    for n in range(NBLK // 2):
        blk = side * (NBLK // 2) + n
        parent = exc_ref[1:2, blk * BLOCK:(blk + 1) * BLOCK]
        oa_s[n:n + 1, :] = jnp.where(lane == parent, 1.0, 0.0).astype(F32)
    oa_ref[...] = oa_s[...].astype(BF16)
    sub_b = lax.broadcasted_iota(jnp.int32, (V, 2 * BLOCK), 0)
    half = lax.broadcasted_iota(jnp.int32, (8, 2 * BLOCK), 1) // BLOCK
    upper = lax.broadcasted_iota(jnp.int32, (8, 2 * BLOCK), 0) // STATES

    def quad(q, _):
        parts = []
        for h in range(2):
            where = pl.ds(pl.multiple_of((side * QUADS * 2 + 2 * q + h) * 2 * BLOCK, 2 * BLOCK), 2 * BLOCK)
            j_row, b_row = exc_ref[2:3, where], exc_ref[3:4, where]
            c4 = coef_ref[:, where]
            c_hi, c_lo = split(jnp.concatenate([c4, c4], axis=0))
            own = half == upper
            q_hi = jnp.where(own, c_hi.astype(F32), 0.0)
            q_lo = jnp.where(own, c_lo.astype(F32), 0.0)
            pick_b = jnp.where(sub_b == b_row, 1.0, 0.0).astype(BF16)
            w_hi, w_lo = [], []
            for jp in range(JP):
                m0, m1 = j_row == 2 * jp, j_row == 2 * jp + 1
                w_hi.append(jnp.concatenate([jnp.where(m0, q_hi, 0.0), jnp.where(m1, q_hi, 0.0)], axis=0).astype(BF16))
                w_lo.append(jnp.concatenate([jnp.where(m0, q_lo, 0.0), jnp.where(m1, q_lo, 0.0)], axis=0).astype(BF16))
            parts.append(dot(jnp.concatenate(w_hi, axis=0), pick_b, NT) + dot(jnp.concatenate(w_lo, axis=0), pick_b, NT))
        high = pl.ds(pl.multiple_of(q * 16, 16), 16)
        low = pl.ds(pl.multiple_of(QUADS * 16 + q * 16, 16), 16)
        for j in range(NEL):
            both = jnp.concatenate([parts[0][j * 8:(j + 1) * 8], parts[1][j * 8:(j + 1) * 8]], axis=0)
            hi, lo = split(both)
            spread_ref[high, j * V:(j + 1) * V] = hi
            spread_ref[low, j * V:(j + 1) * V] = lo
        return _

    lax.fori_loop(0, QUADS, quad, 0, unroll=2)


def value_kernel(me_ref, t0, t1, t2, t3, t4, t5, t6, t7, half0, half1, oa0, oa1, exc_ref, coef_ref,
                 part_ref, tab_ref, p_ref, tia_ref, v_s, x_s, acc_s, exc_smem, sem):
    indices = pltpu.make_async_copy(exc_ref.at[0:1, :], exc_smem, sem)
    indices.start()
    x, c = lax.shift_right_logical(me_ref[1], 1), jnp.bitwise_and(me_ref[1], 1)
    ahead = 1 - 2 * c
    sources = ((x, c), (x - ahead, c), (x + ahead, c), (x + 2, c),
               (x, 1 - c), (x + ahead, 1 - c), (x - ahead, 1 - c), (x + 2, 1 - c))
    for t_ref, (xx, cc) in zip((t0, t1, t2, t3, t4, t5, t6, t7), sources):
        source = 2 * jnp.bitwise_and(xx + 4, 3) + cc
        tab_ref[pl.ds(pl.multiple_of(source * OWN, OWN), OWN), :] = t_ref[...]
    for j in range(NEL, JPAD):
        v_s[pl.ds(j, NBLK, stride=JPAD), :] = jnp.zeros((NBLK, GROUP), F32)
    rows = QUADS * 16
    for side, half in enumerate((half0, half1)):
        x = dot(half[...], tab_ref[...], NT)
        x_s[side * rows:(side + 1) * rows, :] = x[0:rows] + x[rows:]
    pick_a = jnp.concatenate([oa0[...], oa1[...]], axis=0)
    for j in range(NEL):
        v_s[pl.ds(j, NBLK, stride=JPAD), :] = dot(pick_a, tab_ref[:, j * V:(j + 1) * V], NT)

    indices.wait()

    def own_entry(blk, _):
        row = v_s[pl.ds(blk * JPAD + exc_smem[0, blk * BLOCK], 1), :]
        tia_ref[pl.ds(pl.multiple_of(blk * 8, 8), 8), :] = jnp.broadcast_to(row, (8, GROUP))
        return _

    lax.fori_loop(0, NBLK, own_entry, 0, unroll=8)
    acc_s[...] = jnp.zeros_like(acc_s)
    low = lax.broadcasted_iota(jnp.int32, (8, GROUP), 0) < STATES
    sub_b = lax.broadcasted_iota(jnp.int32, (V, BLOCK), 0)
    sub_j = lax.broadcasted_iota(jnp.int32, (JPAD, BLOCK), 0)

    def pair(p, first):
        products = []
        for h in range(2):
            blk = 2 * p + h
            dets = pl.ds(pl.multiple_of(blk * BLOCK, BLOCK), BLOCK)
            pick_j = jnp.where(sub_j == exc_ref[2:3, dets], 1.0, 0.0).astype(BF16)
            pick_b = jnp.where(sub_b == exc_ref[3:4, dets], 1.0, 0.0).astype(BF16)
            t_i = tab_ref[:, pl.ds(pl.multiple_of(exc_smem[0, blk * BLOCK] * V, V), V)]
            along = dot(t_i, pick_b)
            column = v_s[pl.ds(pl.multiple_of(blk * JPAD, JPAD), JPAD), :].astype(BF16)
            down = dot(column, pick_j, TN)
            product = along * down
            hi, lo = split(product)
            p_ref[0:GROUP, dets] = hi
            p_ref[GROUP:2 * GROUP, dets] = lo
            products.append((product, dets))
        for s in range(STATES):
            acc_s[s] += products[0][0] * coef_ref[s:s + 1, products[0][1]] + products[1][0] * coef_ref[s:s + 1, products[1][1]]
        tia = jnp.where(low, tia_ref[pl.ds(pl.multiple_of(p * 16, 16), 8), :],
                        tia_ref[pl.ds(pl.multiple_of(p * 16 + 8, 8), 8), :])
        return first + x_s[pl.ds(pl.multiple_of(p * 8, 8), 8), :] * tia

    first = lax.fori_loop(0, PAIRS, pair, jnp.zeros((8, GROUP), F32), unroll=UNROLL)
    first = first + jnp.concatenate([first[STATES:], first[:STATES]], axis=0)
    second = jnp.concatenate([jnp.sum(acc_s[s].T, axis=0, keepdims=True) for s in range(STATES)] * 2, axis=0)
    part_ref[...] = first - second


def grad_kernel(me_ref, p0, p1, p2, p3, energy_ref, exc_ref, tab_ref, p_ref, tia_ref, own_ref, out_ref, g_s, order_s):
    me = me_ref[1]
    for d, part in enumerate((p0, p1, p2, p3)):
        order_s[jnp.bitwise_and(lax.shift_right_logical(me, 1) - d + 4, 3)] = part[...]
    val = (order_s[0] + order_s[1]) + (order_s[2] + order_s[3])
    own = val[0:STATES, 0:OWN]
    for d in range(1, NDET):
        own = jnp.where(me == d, val[0:STATES, d * OWN:(d + 1) * OWN], own)
    own_ref[...] = own
    low = lax.broadcasted_iota(jnp.int32, (8, GROUP), 0) < STATES
    lane = lax.broadcasted_iota(jnp.int32, (8, GROUP), 1)
    square = val * val
    guide = 1.0 + jnp.sum(jnp.where(low, square, 0.0), axis=0, keepdims=True)
    energy = jnp.concatenate([energy_ref[...], energy_ref[...]], axis=0)
    middle = jnp.sum(energy, axis=1, keepdims=True) * (1.0 / GROUP)
    scaled = val / guide
    weight = square / guide
    sums = jnp.sum(jnp.where(low, weight, weight * energy), axis=1, keepdims=True)
    meta = jnp.zeros((8, GROUP), F32)
    for at, value in ((0, sums), (3, middle)):
        for n in range(3):
            piece = value.astype(BF16).astype(F32)
            meta = jnp.where(lane == at + n, piece, meta)
            value = value - piece
    meta = jnp.concatenate([meta, meta], axis=0).astype(BF16)
    factor = jnp.where(low, scaled * (energy - middle), scaled)
    f_hi, f_lo = split(factor)
    f16 = jnp.concatenate([f_hi.astype(F32), f_lo.astype(F32)], axis=0).astype(BF16)
    f16 = jnp.concatenate([f16, f16], axis=1)
    lhs = tia_ref[...].reshape(NBLK, 8, GROUP) * factor[None]
    l_hi, l_lo = split(lhs.reshape(NBLK * 8, GROUP))
    lhs = jnp.concatenate([l_hi, l_lo], axis=1)

    for jp in range(JP):
        t = tab_ref[:, jp * 2 * V:(jp + 1) * 2 * V]
        g = dot(lhs, jnp.concatenate([t, t], axis=0)).reshape(NBLK, 8, 2 * V)
        hi, lo = split(jnp.concatenate([g[:, :, 0:V], g[:, :, V:2 * V]], axis=1))
        g_s[:, jp * 16:(jp + 1) * 16, 0:V] = hi
        g_s[:, jp * 16:(jp + 1) * 16, V:2 * V] = lo
    sub_b = lax.broadcasted_iota(jnp.int32, (V, BLOCK), 0)

    def slot(p, _):
        both = pl.ds(pl.multiple_of(p * 2 * BLOCK, 2 * BLOCK), 2 * BLOCK)
        second = dot(f16, p_ref[:, both])
        second = second[0:8] + second[8:16]
        terms = []
        for h in range(2):
            dets = pl.ds(pl.multiple_of(p * 2 * BLOCK + h * BLOCK, BLOCK), BLOCK)
            j_row, b_row = exc_ref[2:3, dets], exc_ref[3:4, dets]
            pick_b = jnp.where(sub_b == b_row, 1.0, 0.0).astype(BF16)
            y = dot(g_s[2 * p + h], jnp.concatenate([pick_b, pick_b], axis=0))
            first = jnp.zeros((8, BLOCK), F32)
            for j in range(NEL):
                first = jnp.where(j_row == j, y[j * 8:(j + 1) * 8], first)
            terms.append(first - second[:, h * BLOCK:(h + 1) * BLOCK])
        out_ref[p, :, 0:BLOCK] = jnp.concatenate(terms, axis=0).astype(BF16)
        out_ref[p, :, BLOCK:2 * BLOCK] = meta
        return _

    lax.fori_loop(0, NWALK, slot, 0, unroll=UNROLL)


def final_kernel(in_ref, grad_ref, energy_ref):
    lane = lax.broadcasted_iota(jnp.int32, (8, BLOCK), 1)
    metas = [in_ref[g].astype(F32)[0:8, BLOCK:2 * BLOCK] for g in range(NWALK)]
    meta = metas[0]
    for g in range(1, NWALK):
        meta = meta + metas[g]
    sums = jnp.sum(jnp.where(lane < 3, meta, 0.0), axis=1, keepdims=True)
    total, weighted = sums[0:STATES], sums[STATES:8]
    energy = weighted / total
    grads = [jnp.zeros((STATES, BLOCK), F32)] * 2
    for g in range(NWALK):
        terms = in_ref[g].astype(F32)
        middle = jnp.sum(jnp.where((lane >= 3) & (lane < 6), metas[g], 0.0), axis=1, keepdims=True)
        shift = middle[0:STATES] - energy
        for h in range(2):
            grads[h] = grads[h] + (terms[h * 8:h * 8 + STATES, 0:BLOCK]
                                   + shift * terms[h * 8 + STATES:h * 8 + 8, 0:BLOCK])
    scale = 2.0 / total
    grad_ref[:, 0, 0:BLOCK] = grads[0] * scale
    grad_ref[:, 0, BLOCK:2 * BLOCK] = grads[1] * scale
    place = lax.broadcasted_iota(jnp.int32, (STATES, STATES), 0) == lax.broadcasted_iota(jnp.int32, (STATES, STATES), 1)
    energy_ref[...] = jnp.sum(jnp.where(place, energy, 0.0), axis=0, keepdims=True)


def params(mib):
    return pltpu.CompilerParams(vmem_limit_bytes=mib * MIB)


def make_table(positions, inverse, centers, exponent, orbital_weights):
    return pl.pallas_call(
        table_kernel,
        out_shape=jax.ShapeDtypeStruct((OWN, NEL * V), BF16),
        in_specs=[pl.BlockSpec(memory_space=pltpu.HBM)] * 5, out_specs=vmem(1)[0],
        scratch_shapes=[pltpu.VMEM((3, OWN, NEL), F32), pltpu.VMEM((NEL, OWN, NEL), F32), pltpu.VMEM((3, NBAS), F32),
                        pltpu.VMEM((1, NBAS), F32), pltpu.VMEM((NBAS, V), F32), pltpu.VMEM((128, 128), F32), pltpu.VMEM((OWN * ROWS, NBAS), F32),
                        pltpu.VMEM((OWN, 128, V), F32), pltpu.VMEM((OWN, JPAD, 128), F32),
                        pltpu.VMEM((ROWS * OWN, V), F32), pltpu.SemaphoreType.DMA((5,))],
        compiler_params=params(60), name="tables",
    )(positions, inverse.transpose(1, 0, 2), centers, exponent.reshape(1, NBAS), orbital_weights)


def cost(flops):
    return pl.CostEstimate(flops=flops, bytes_accessed=8 * MIB, transcendentals=0)


def spread_first(excitations, coeffs):
    return pl.pallas_call(
        first_kernel,
        out_shape=[jax.ShapeDtypeStruct((QUADS * 32, NEL * V), BF16), jax.ShapeDtypeStruct((NBLK // 2, V), BF16),
                   jax.ShapeDtypeStruct((4, KD), jnp.int32), jax.ShapeDtypeStruct((4, KD), F32)],
        in_specs=vmem(2), out_specs=vmem(4),
        scratch_shapes=[pltpu.VMEM((NBLK // 2, V), F32)],
        compiler_params=params(8), cost_estimate=cost(50_000_000), name="spread_first",
    )(excitations, coeffs)


def spread(side, excitations, coeffs):
    return pl.pallas_call(
        functools.partial(spread_kernel, side),
        out_shape=[jax.ShapeDtypeStruct((QUADS * 32, NEL * V), BF16), jax.ShapeDtypeStruct((NBLK // 2, V), BF16)],
        in_specs=vmem(2), out_specs=vmem(2),
        scratch_shapes=[pltpu.VMEM((NBLK // 2, V), F32)],
        compiler_params=params(8), cost_estimate=cost(50_000_000), name="spread",
    )(excitations, coeffs)


def partial_values(me, tables, halves, columns, excitations, coeffs):
    return pl.pallas_call(
        value_kernel,
        out_shape=[jax.ShapeDtypeStruct((8, GROUP), F32), jax.ShapeDtypeStruct((GROUP, NEL * V), BF16),
                   jax.ShapeDtypeStruct((2 * GROUP, KD), BF16), jax.ShapeDtypeStruct((NBLK * 8, GROUP), F32)],
        in_specs=[pl.BlockSpec(memory_space=pltpu.SMEM)] + vmem(NDET + 6), out_specs=vmem(4),
        scratch_shapes=[pltpu.VMEM((NBLK * JPAD, GROUP), F32), pltpu.VMEM((NBLK * STATES, GROUP), F32),
                        pltpu.VMEM((STATES, GROUP, BLOCK), F32),
                        pltpu.SMEM((1, KD), jnp.int32), pltpu.SemaphoreType.DMA],
        compiler_params=params(22), name="partial_values",
    )(me, *tables, *halves, *columns, excitations, coeffs)


def gradient(me, parts, local_energy, excitations, tab, pair_products, tia):
    return pl.pallas_call(
        grad_kernel,
        out_shape=[jax.ShapeDtypeStruct((STATES, OWN), F32), jax.ShapeDtypeStruct((NWALK, 16, 2 * BLOCK), BF16)],
        in_specs=[pl.BlockSpec(memory_space=pltpu.SMEM)] + vmem(9), out_specs=vmem(2),
        scratch_shapes=[pltpu.VMEM((NBLK, JP * 16, 2 * V), BF16), pltpu.VMEM((4, 8, GROUP), F32)],
        compiler_params=params(20), name="gradient",
    )(me, *parts, local_energy, excitations, tab, pair_products, tia)


def finish(messages):
    return pl.pallas_call(
        final_kernel,
        out_shape=[jax.ShapeDtypeStruct((STATES, 1, 256), F32), jax.ShapeDtypeStruct((1, STATES), F32)],
        in_specs=vmem(1), out_specs=vmem(2),
        compiler_params=params(8), name="finish",
    )(messages)


def across(x, step):
    return lax.ppermute(x, "det", [(i, (i + 2 * step(i % 2)) % NDET) for i in range(NDET)])


def other_core(x):
    return lax.ppermute(x, "det", [(i, i ^ 1) for i in range(NDET)])


def shards(positions, inverse, centers, exponent, orbital_weights, excitations, state_coeffs, local_energy):
    me = jnp.stack([lax.axis_index("walk"), lax.axis_index("det")])
    table = make_table(positions, inverse, centers, exponent, orbital_weights)
    ahead = across(table, lambda c: 1 - 2 * c)
    behind = across(table, lambda c: 2 * c - 1)
    half0, columns0, excitations, state_coeffs = spread_first(excitations, state_coeffs)
    ahead, columns0 = lax.optimization_barrier((ahead, columns0))
    beyond = across(ahead, lambda c: 1 - 2 * c)
    half1, columns1 = spread(1, excitations, state_coeffs)
    near = [other_core(t) for t in (table, ahead, behind)]
    tables = [table, ahead, behind, beyond] + near + [other_core(beyond)]
    part, tab, products, tia = partial_values(me, tables, (half0, half1), (columns0, columns1), excitations, state_coeffs)
    chip = part + other_core(part)
    parts = [chip] + [across(chip, lambda c, d=d: d) for d in (1, 2, 3)]
    own, messages = gradient(me, parts, local_energy, excitations, tab, products, tia)
    grad, energy = finish(lax.all_to_all(messages, "walk", 0, 0, tiled=True))
    return grad, own, energy.reshape(STATES)


def solution(mesh):
    in_specs = (
        P(None, ("walk", "det"), None),
        P(("walk", "det"), None, None),
        P(),
        P(),
        P(),
        P(None, "det"),
        P(None, "det"),
        P(None, "walk"),
    )
    out_specs = (P(None, "det", "walk"), P(None, ("walk", "det")), P())
    return jax.shard_map(shards, mesh=mesh, in_specs=in_specs, out_specs=out_specs, check_vma=False)
```
